256 devices in a mesh: group: 8 (over z), patch: 32 (over x, y, core).
Axes of the slice: x: 4, y: 4, z: 8, core: 2. Of those that a mesh axis runs over, the one named last changes fastest.
Arguments:
- node_lat: bfloat16 [131072, 512], P(('group', 'patch')), may hold values from -6 to 6
- fine_edge_lat: bfloat16 [262144, 512], P(('group', 'patch')), may hold values from -6 to 6
- fine_send: int32 [262144], P(('group', 'patch')), may hold values from 0 to 767
- fine_recv: int32 [262144], P(('group', 'patch')), may hold values from 0 to 511
- border_rows: int32 [65536], P(('group', 'patch')), may hold values from 0 to 511
- coarse_edge_lat: bfloat16 [32768, 512], P('patch'), may hold values from -6 to 6
- coarse_send: int32 [32768], P('patch'), may hold values from 0 to 2047
- coarse_recv: int32 [32768], P('patch'), may hold values from 0 to 2047
- w_edge_in: bfloat16 [1536, 512], replicated, may hold values from -0.15625 to 0.15625
- w_edge_out: bfloat16 [512, 512], replicated, may hold values from -0.25 to 0.25
- edge_gain: float32 [512], replicated, may hold values from 0.25 to 1.75
- w_node_in: bfloat16 [1024, 512], replicated, may hold values from -0.1875 to 0.1875
- w_node_out: bfloat16 [512, 512], replicated, may hold values from -0.25 to 0.25
- node_gain: float32 [512], replicated, may hold values from 0.25 to 1.75
Outputs:
- node_new: bfloat16 [131072, 512], P(('group', 'patch'))
- fine_edge_new: bfloat16 [262144, 512], P(('group', 'patch'))
- coarse_edge_new: bfloat16 [32768, 512], P('patch')
The draws below stay inside these ranges and needn't reach their ends.
All inputs are finite; a program needn't handle non-finite values.
Results may differ from the reference program's by a relative error of at most 0.0052.
Values may be sent and summed in bfloat16 or wider, within the bound.
No kernel may reach another device: no remote copies, remote signals or barrier semaphores. Data moves between devices by JAX's collectives and lax.ppermute only.
A program may use at most 64 MiB of HBM per device.

```python
import math
import jax
import jax.numpy as jnp
import numpy as np
from jax import lax

D = 512
NODE_DEV = 512
FEDGE_DEV = 1024
BORDER = 128
CM_DEV = 8
EXT = 768
NODES = 131072
FEDGES = 262144
COARSE = 2048
CEDGES = 32768
N_GROUP = 8
N_PATCH = 32
DEVICES = 256


def set_ends(result, key, smallest, top_value):
    extent = result.shape
    spot = [jax.random.randint(jax.random.fold_in(key, axis), (), 0, extent[axis]) for axis in range(len(extent))]
    result = result.at[tuple(spot)].set(smallest)
    longest = extent.index(max(extent))
    spot[longest] = (spot[longest] + 1) % extent[longest]
    return result.at[tuple(spot)].set(top_value)


def steps_of(own_key, dims, cuts, low, top_value):
    factor_of, own = 1.0, jax.random.fold_in(own_key, 6)
    for axis_at, parts in cuts:
        heights = jnp.exp(jax.random.uniform(jax.random.fold_in(own, axis_at), (parts,), jnp.float32, low / len(cuts), top_value / len(cuts)))
        factor_of = factor_of * jnp.repeat(heights, dims[axis_at] // parts).reshape([-1 if axis == axis_at else 1 for axis in range(len(dims))])
    return factor_of


def cumulative_ranks(amount, skew):
    loads = [(1 << 20) // math.isqrt(grade ** skew) + 1 for grade in range(1, amount + 1)]
    deviation = 1 + sum(loads) // (1 << 30)
    return np.cumsum(np.array([max(1, weight // deviation) for weight in loads]))


def ranked_ids(key, shape, number_of, slope):
    table = cumulative_ranks(number_of, slope)
    pick = jax.random.randint(jax.random.fold_in(key, 1), shape, 0, int(table[number_of - 1]))
    rank = jnp.searchsorted(jnp.asarray(table, jnp.int32), pick, side="right")
    return jax.random.permutation(jax.random.fold_in(key, 2), number_of)[rank].astype(jnp.int32)


def bell_draw(stream_key, extent, width, most, split=(), kind=jnp.bfloat16):
    result = width * jax.random.normal(stream_key, extent, jnp.float32)
    if split:
        result = result * steps_of(stream_key, extent, split, -0.22, 0.18)
    return jnp.clip(result, -most, most).astype(kind)


def setup_inputs(seed: int = 0) -> dict:
    key_list = jax.random.split(jax.random.key(seed), 15)
    return {
        "node_lat": bell_draw(key_list[0], (NODES, D), 1.0, 6.0, ((0, 256),)),
        "fine_edge_lat": bell_draw(key_list[1], (FEDGES, D), 1.0, 6.0, ((0, 256),)),
        "fine_send": set_ends(jax.random.randint(key_list[2], (FEDGES,), 0, EXT), jax.random.fold_in(key_list[2], 1), 0, EXT - 1).astype(jnp.int32),
        "fine_recv": set_ends(jax.random.randint(key_list[3], (FEDGES,), 0, NODE_DEV), jax.random.fold_in(key_list[3], 1), 0, NODE_DEV - 1).astype(jnp.int32),
        "border_rows": set_ends(jax.random.randint(key_list[4], (DEVICES * 2 * BORDER,), 0, NODE_DEV), jax.random.fold_in(key_list[4], 1), 0, NODE_DEV - 1).astype(jnp.int32),
        "coarse_edge_lat": bell_draw(key_list[5], (CEDGES, D), 1.0, 6.0, ((0, 32),)),
        "coarse_send": set_ends(jax.random.randint(key_list[6], (CEDGES,), 0, COARSE), jax.random.fold_in(key_list[6], 1), 0, COARSE - 1).astype(jnp.int32),
        "coarse_recv": set_ends(ranked_ids(key_list[7], (CEDGES,), COARSE, 2), jax.random.fold_in(key_list[7], 3), 0, COARSE - 1).astype(jnp.int32),
        "w_edge_in": bell_draw(key_list[8], (3 * D, D), (3 * D) ** -0.5, 0.15625),
        "w_edge_out": bell_draw(key_list[9], (D, D), D ** -0.5, 0.25),
        "edge_gain": jnp.clip(1.0 + 0.15 * jax.random.normal(key_list[10], (D,), jnp.float32), 0.25, 1.75),
        "w_node_in": bell_draw(key_list[11], (2 * D, D), (2 * D) ** -0.5, 0.1875),
        "w_node_out": bell_draw(key_list[12], (D, D), D ** -0.5, 0.25),
        "node_gain": jnp.clip(1.0 + 0.15 * jax.random.normal(key_list[13], (D,), jnp.float32), 0.25, 1.75),
    }


def layer_norm(values):
    average = lax.optimization_barrier(jnp.mean(values, axis=-1, keepdims=True))
    centred = values - average
    variance = lax.optimization_barrier(jnp.mean(centred * centred, axis=-1, keepdims=True))
    return centred * lax.rsqrt(variance + 1e-05)

def edge_update(edges, senders, receivers, w_edge_in, w_edge_out, edge_gain):
    model_width = edges.shape[1]
    preact = jnp.dot(edges, w_edge_in[:model_width], preferred_element_type=jnp.float32)
    preact = preact + jnp.dot(senders, w_edge_in[model_width:2 * model_width], preferred_element_type=jnp.float32)
    preact = preact + jnp.dot(receivers, w_edge_in[2 * model_width:], preferred_element_type=jnp.float32)
    hidden = jax.nn.silu(preact).astype(jnp.bfloat16)
    projected = jnp.dot(hidden, w_edge_out, preferred_element_type=jnp.float32)
    return (edges.astype(jnp.float32) + layer_norm(projected) * edge_gain).astype(jnp.bfloat16)

def reference(node_lat, fine_edge_lat, fine_send, fine_recv, border_rows, coarse_edge_lat, coarse_send, coarse_recv, w_edge_in, w_edge_out, edge_gain, w_node_in, w_node_out, node_gain):
    model_width = node_lat.shape[1]
    node_four = node_lat.reshape(N_GROUP, N_PATCH, NODE_DEV, model_width)
    border_four = border_rows.reshape(N_GROUP, N_PATCH, 2 * BORDER).astype(jnp.int32)
    picked = jnp.take_along_axis(node_four, border_four[..., None], axis=2)
    picked = picked.reshape(N_GROUP, N_PATCH, 2, BORDER, model_width)
    low_halo = jnp.roll(picked[:, :, 1], 1, axis=1)
    high_halo = jnp.roll(picked[:, :, 0], -1, axis=1)
    extended = jnp.concatenate([node_four, low_halo, high_halo], axis=2).reshape(DEVICES, EXT, model_width)
    own_nodes = node_lat.reshape(DEVICES, NODE_DEV, model_width)
    edges_three = fine_edge_lat.reshape(DEVICES, FEDGE_DEV, model_width)
    send_two = fine_send.reshape(DEVICES, FEDGE_DEV)
    recv_two = fine_recv.reshape(DEVICES, FEDGE_DEV)

    def one_device(operands):
        ext_rows, mine, edges, senders, receivers = operands
        renewed = edge_update(edges, ext_rows[senders], mine[receivers], w_edge_in, w_edge_out, edge_gain)
        summed = jax.ops.segment_sum(renewed.astype(jnp.float32), receivers, num_segments=NODE_DEV)
        return (renewed, summed)
    fine_new, fine_sum = lax.map(one_device, (extended, own_nodes, edges_three, send_two, recv_two))
    coarse_table = own_nodes[:, :CM_DEV].reshape(COARSE, model_width)
    coarse_new = edge_update(coarse_edge_lat, coarse_table[coarse_send], coarse_table[coarse_recv], w_edge_in, w_edge_out, edge_gain)
    coarse_sum = jax.ops.segment_sum(coarse_new.astype(jnp.float32), coarse_recv, num_segments=COARSE)
    summed_all = fine_sum.at[:, :CM_DEV].add(coarse_sum.reshape(DEVICES, CM_DEV, model_width))
    incoming = summed_all.reshape(NODES, model_width).astype(jnp.bfloat16)
    preact = jnp.dot(node_lat, w_node_in[:model_width], preferred_element_type=jnp.float32)
    preact = preact + jnp.dot(incoming, w_node_in[model_width:], preferred_element_type=jnp.float32)
    node_hidden = jax.nn.silu(preact).astype(jnp.bfloat16)
    projected = jnp.dot(node_hidden, w_node_out, preferred_element_type=jnp.float32)
    node_new = (node_lat.astype(jnp.float32) + layer_norm(projected) * node_gain).astype(jnp.bfloat16)
    return (node_new, fine_new.reshape(FEDGES, model_width), coarse_new)
```

```python
import jax
import jax.numpy as jnp
from jax import lax
from jax.experimental import pallas as pl
from jax.experimental.pallas import tpu as pltpu
from jax.sharding import PartitionSpec as P

D = 512
GROUPS = 8
SIDE = 4
CORES = 2
PATCHES = SIDE * SIDE * CORES
BORDER = 128
COARSE_ROWS = 8
EDGES = 1024
NODES = 512
EPS = 1e-05
BF = jnp.bfloat16
F32 = jnp.float32
BLOCK = 256
VMEM_LIMIT = 24 * 1024 * 1024


def dot(a, b):
    return jnp.dot(a, b, preferred_element_type=F32)


def silu(values):
    half = 0.5 * values
    return half * jnp.tanh(half) + half


def layer_norm(values):
    average = jnp.mean(values, axis=-1, keepdims=True)
    centred = values - average
    variance = jnp.mean(centred * centred, axis=-1, keepdims=True)
    return centred * lax.rsqrt(variance + EPS)


def column_of(ids_ref, first, rows):
    tiles = []
    for at in range(first // 128, (first + rows) // 128):
        row = jnp.broadcast_to(ids_ref[at : at + 1, :], (128, 128))
        tiles.append(row.T)
    return jnp.concatenate(tiles, axis=0).astype(jnp.int16)


def one_hot(column, width, offset=0):
    lanes = lax.broadcasted_iota(jnp.int16, column.shape, 1)
    one, zero = jnp.ones(column.shape, BF), jnp.zeros(column.shape, BF)
    return jnp.concatenate(
        [
            jnp.where(column == lanes + jnp.int16(offset + 128 * at), one, zero)
            for at in range(width // 128)
        ],
        axis=1,
    )


def one_hot_rows(ids_ref, count, height):
    rows = lax.broadcasted_iota(jnp.int16, (height, 128), 0)
    one, zero = jnp.ones((height, 128), BF), jnp.zeros((height, 128), BF)
    parts = []
    for at in range(count // 128):
        ids = jnp.broadcast_to(ids_ref[at : at + 1, :], (height, 128)).astype(jnp.int16)
        parts.append(jnp.where(ids == rows, one, zero))
    return jnp.concatenate(parts, axis=1)


def finish_edges(pre, edges, w_out, gain):
    hidden = silu(pre).astype(BF)
    projected = dot(hidden, w_out)
    return (edges.astype(F32) + layer_norm(projected) * gain).astype(BF)


def pick_kernel(node_ref, border_ref, low_ref, high_ref):
    hot = one_hot(column_of(border_ref, 0, 2 * BORDER), NODES)
    picked = dot(hot, node_ref[...]).astype(BF)
    low_ref[...] = picked[:BORDER]
    high_ref[...] = picked[BORDER:]


def project_kernel(node_ref, w_ref, out_ref):
    nodes = node_ref[...]
    out_ref[:NODES] = dot(nodes, w_ref[2 * D :]).astype(BF)
    out_ref[NODES:] = dot(nodes, w_ref[D : 2 * D]).astype(BF)


def fine_kernel(
    edge_ref, send_ref, recv_ref, table_ref, low_ref, high_ref, w_in_ref, w_out_ref, gain_ref,
    new_ref, sum_ref, halo_ref,
):
    halo_ref[:BORDER] = dot(low_ref[...], w_in_ref[D : 2 * D]).astype(BF)
    halo_ref[BORDER:] = dot(high_ref[...], w_in_ref[D : 2 * D]).astype(BF)
    gain = gain_ref[...]
    for first in range(0, EDGES, BLOCK):
        rows = slice(first, first + BLOCK)
        edges = edge_ref[rows]
        recv_hot = one_hot(column_of(recv_ref, first, BLOCK), NODES)
        send_hot = one_hot(column_of(send_ref, first, BLOCK), NODES + 2 * BORDER)
        pre = dot(edges, w_in_ref[:D])
        pre = pre + dot(recv_hot, table_ref[:NODES])
        pre = pre + dot(send_hot[:, :NODES], table_ref[NODES:])
        pre = pre + dot(send_hot[:, NODES:], halo_ref[...])
        new_ref[rows] = finish_edges(pre, edges, w_out_ref[...], gain)
    sum_ref[...] = dot(one_hot_rows(recv_ref, EDGES, NODES), new_ref[...])


def gather_kernel(send_ref, recv_ref, table_ref, send_out, recv_out):
    for first in range(0, EDGES, BLOCK):
        rows = slice(first, first + BLOCK)
        for ids_ref, out_ref in ((send_ref, send_out), (recv_ref, recv_out)):
            hot = one_hot(column_of(ids_ref, first, BLOCK), table_ref.shape[0])
            out_ref[rows] = dot(hot, table_ref[...]).astype(BF)


def coarse_kernel(
    edge_ref, send_ref, recv_ref, slot_ref, table_ref, send_part, recv_part, w_in_ref, w_out_ref,
    gain_ref, new_ref, mine_ref, theirs_ref,
):
    gain = gain_ref[...]
    half = table_ref.shape[0]
    for first in range(0, EDGES, BLOCK):
        rows = slice(first, first + BLOCK)
        edges = edge_ref[rows]
        pre = dot(edges, w_in_ref[:D])
        for ids_ref, part_ref, at in ((send_ref, send_part, 1), (recv_ref, recv_part, 2)):
            hot = one_hot(column_of(ids_ref, first, BLOCK), half, half)
            picked = (dot(hot, table_ref[...]) + part_ref[rows].astype(F32)).astype(BF)
            pre = pre + dot(picked, w_in_ref[at * D : (at + 1) * D])
        new_ref[rows] = finish_edges(pre, edges, w_out_ref[...], gain)
    height = 2 * mine_ref.shape[0]
    sums = dot(one_hot_rows(slot_ref, EDGES, height), new_ref[...])
    mine_ref[...] = sums[: height // 2]
    theirs_ref[...] = sums[height // 2 :].astype(BF)


def node_rows(nodes, incoming, w_in_ref, w_out_ref, gain):
    pre = dot(nodes, w_in_ref[:D]) + dot(incoming, w_in_ref[D:])
    projected = dot(silu(pre).astype(BF), w_out_ref[...])
    return (nodes.astype(F32) + layer_norm(projected) * gain).astype(BF)


def node_kernel(node_ref, sum_ref, w_in_ref, w_out_ref, gain_ref, out_ref, first_ref):
    for first in range(0, NODES, BLOCK):
        rows = slice(first, first + BLOCK)
        out_ref[rows] = node_rows(
            node_ref[rows], sum_ref[rows].astype(BF), w_in_ref, w_out_ref, gain_ref[...]
        )
    first_ref[...] = sum_ref[: first_ref.shape[0]]


def tail_kernel(
    node_ref, sum_ref, part0, part1, part2, part3, w_in_ref, w_out_ref, gain_ref, _, out_ref
):
    coarse = part0[...] + (
        part1[...].astype(F32) + part2[...].astype(F32) + part3[...].astype(F32)
    )
    total = sum_ref[...]
    total = jnp.concatenate([total[:COARSE_ROWS] + coarse, total[COARSE_ROWS:]], axis=0)
    out_ref[...] = node_rows(node_ref[...], total.astype(BF), w_in_ref, w_out_ref, gain_ref[...])


def shape(rows, dtype=BF):
    return jax.ShapeDtypeStruct((rows, D), dtype)


def call(kernel, outs, flops, *args, scratch=(), name=None):
    return pl.pallas_call(
        kernel,
        out_shape=outs,
        scratch_shapes=scratch,
        compiler_params=pltpu.CompilerParams(vmem_limit_bytes=VMEM_LIMIT),
        cost_estimate=pl.CostEstimate(flops=flops, bytes_accessed=4 << 20, transcendentals=0),
        name=name,
    )(*args)


def patch_pairs(move):
    pairs = []
    for x in range(SIDE):
        for y in range(SIDE):
            for core in range(CORES):
                to_x, to_y, to_core = move(x, y, core)
                pairs.append(
                    ((x * SIDE + y) * CORES + core, (to_x * SIDE + to_y) * CORES + to_core)
                )
    return pairs


def swap_x(k):
    return patch_pairs(lambda x, y, c: (x ^ k, y, c))


def swap_y(k):
    return patch_pairs(lambda x, y, c: (x, y ^ k, c))


def swap_one(k):
    return patch_pairs(lambda x, y, c: (x ^ k, y, c) if c == 0 else (x, y ^ k, c))


def swap_other(k):
    return patch_pairs(lambda x, y, c: (x, y ^ k, c) if c == 0 else (x ^ k, y, c))


SWAP_CORE = patch_pairs(lambda x, y, c: (x, y, c ^ 1))


def shards(
    node_lat, fine_edge_lat, fine_send, fine_recv, border_rows, coarse_edge_lat, coarse_send,
    coarse_recv, w_edge_in, w_edge_out, edge_gain, w_node_in, w_node_out, node_gain,
):
    group = lax.axis_index("group")
    patch = lax.axis_index("patch")
    my_core, my_y, my_x = patch % CORES, patch // CORES % SIDE, patch // (CORES * SIDE)
    edge_gain = edge_gain[None, :]
    node_gain = node_gain[None, :]
    grid = lambda ids: ids.reshape(-1, 128)

    part = node_lat[:COARSE_ROWS]
    for k in (1, 2, 4):
        other = lax.ppermute(part, "group", [(i, i ^ k) for i in range(GROUPS)])
        part = jnp.concatenate([part, other], axis=0)
    for swap in (swap_one, swap_other):
        part = jnp.concatenate(
            [part] + [lax.ppermute(part, "patch", swap(k)) for k in range(1, SIDE)], axis=0
        )
    other_half = lax.ppermute(part, "patch", SWAP_CORE)

    def place(ids):
        row, at = ids % COARSE_ROWS, ids // COARSE_ROWS
        core, y, x = at % CORES, at // CORES % SIDE ^ my_y, at // (CORES * SIDE) % SIDE ^ my_x
        z = at // PATCHES ^ group
        far = jnp.where(core == 0, y, x)
        near = jnp.where(core == 0, x, y)
        return (((core ^ my_core) * SIDE + far) * SIDE + near) * (GROUPS * COARSE_ROWS) + (
            z * COARSE_ROWS + row
        )

    row, at = coarse_recv % COARSE_ROWS, coarse_recv // COARSE_ROWS
    slot = (
        ((at % CORES ^ my_core) * SIDE + (at // (CORES * SIDE) % SIDE ^ my_x)) * SIDE
        + (at // CORES % SIDE ^ my_y)
    ) * COARSE_ROWS + row
    slot = grid(jnp.where(at // PATCHES == group, slot, -1))
    send_place, recv_place = grid(place(coarse_send)), grid(place(coarse_recv))

    low, high = call(
        pick_kernel, (shape(BORDER), shape(BORDER)), 2 * 256 * 512 * 512, node_lat,
        grid(border_rows), name="pick",
    )
    up = [(i, (i + 1) % PATCHES) for i in range(PATCHES)]
    down = [(j, i) for i, j in up]
    from_low = lax.ppermute(high, "patch", up)
    from_high = lax.ppermute(low, "patch", down)

    table = call(
        project_kernel, shape(2 * NODES), 4 * 512 * 512 * 512, node_lat, w_edge_in, name="project"
    )
    fine_new, fine_sum = call(
        fine_kernel, (shape(EDGES), shape(NODES, F32)), 3 << 30, fine_edge_lat, grid(fine_send),
        grid(fine_recv), table, from_low, from_high, w_edge_in, w_edge_out, edge_gain,
        scratch=[pltpu.VMEM((2 * BORDER, D), BF)], name="fine",
    )
    node_main, first_sum = call(
        node_kernel, (shape(NODES), shape(16, F32)), 768 << 20, node_lat, fine_sum, w_node_in,
        w_node_out, node_gain, name="node",
    )

    send_part, recv_part = call(
        gather_kernel, (shape(EDGES), shape(EDGES)), 2 << 30, send_place, recv_place, part,
        name="gather",
    )
    coarse_new, mine, theirs = call(
        coarse_kernel, (shape(EDGES), shape(128, F32), shape(128)), 4 << 30, coarse_edge_lat,
        send_place, recv_place, slot, other_half, send_part, recv_part, w_edge_in, w_edge_out,
        edge_gain, name="coarse",
    )

    total = mine + lax.ppermute(theirs, "patch", SWAP_CORE).astype(F32)
    width = total.shape[0] // SIDE
    sends = total.astype(BF)
    total = total[:width] + sum(
        lax.ppermute(sends[k * width : (k + 1) * width], "patch", swap_x(k)).astype(F32)
        for k in range(1, SIDE)
    )
    sends = total.astype(BF)
    last = [
        lax.ppermute(sends[k * COARSE_ROWS : (k + 1) * COARSE_ROWS], "patch", swap_y(k))
        for k in range(1, SIDE)
    ]

    whole = lambda rows: pl.BlockSpec((rows, D), lambda i: (0, 0))
    node_new = pl.pallas_call(
        tail_kernel,
        grid=(1,),
        out_shape=shape(NODES),
        in_specs=[whole(16), whole(16)] + [whole(COARSE_ROWS)] * 4
        + [whole(2 * D), whole(D), whole(1), pl.BlockSpec(memory_space=pl.ANY)],
        out_specs=whole(16),
        input_output_aliases={9: 0},
        compiler_params=pltpu.CompilerParams(vmem_limit_bytes=VMEM_LIMIT),
        name="tail",
    )(node_lat, first_sum, total[:COARSE_ROWS], *last, w_node_in, w_node_out, node_gain, node_main)
    return (node_new, fine_new, coarse_new)


def solution(mesh):
    in_specs = (
        P(("group", "patch"), None), P(("group", "patch"), None), P(("group", "patch")),
        P(("group", "patch")), P(("group", "patch")), P("patch", None), P("patch"), P("patch"),
        P(), P(), P(), P(), P(), P(),
    )
    out_specs = (P(("group", "patch"), None), P(("group", "patch"), None), P("patch", None))
    return jax.shard_map(shards, mesh=mesh, in_specs=in_specs, out_specs=out_specs, check_vma=False)
```

```python
import functools

import jax
import jax.numpy as jnp
from jax import lax
from jax.experimental import pallas as pl
from jax.experimental.pallas import tpu as pltpu
from jax.sharding import PartitionSpec as P

D = 512
GROUPS = 8
SIDE = 4
CORES = 2
PATCHES = SIDE * SIDE * CORES
BORDER = 128
COARSE_ROWS = 8
EDGES = 1024
HALF = 512
NODES = 512
TAIL = 16
EPS = 1e-05
BF = jnp.bfloat16
F32 = jnp.float32
BLOCK = 256
VMEM_LIMIT = 24 * 1024 * 1024


def dot(a, b):
    return jnp.dot(a, b, preferred_element_type=F32)


def silu(values):
    half = 0.5 * values
    return half * jnp.tanh(half) + half


def layer_norm(values):
    average = jnp.mean(values, axis=-1, keepdims=True)
    centred = values - average
    variance = jnp.mean(centred * centred, axis=-1, keepdims=True)
    return centred * lax.rsqrt(variance + EPS)


def column_of(ids_ref, first, rows):
    tiles = []
    for at in range(first // 128, (first + rows) // 128):
        row = jnp.broadcast_to(ids_ref[at : at + 1, :], (128, 128))
        tiles.append(row.T)
    return jnp.concatenate(tiles, axis=0).astype(jnp.int16)


def one_hot(column, width, offset=0):
    lanes = lax.broadcasted_iota(jnp.int16, column.shape, 1)
    one, zero = jnp.ones(column.shape, BF), jnp.zeros(column.shape, BF)
    return jnp.concatenate(
        [
            jnp.where(column == lanes + jnp.int16(offset + 128 * at), one, zero)
            for at in range(width // 128)
        ],
        axis=1,
    )


def one_hot_rows(ids_ref, first, count, height):
    rows = lax.broadcasted_iota(jnp.int16, (height, 128), 0)
    one, zero = jnp.ones((height, 128), BF), jnp.zeros((height, 128), BF)
    parts = []
    for at in range(first // 128, (first + count) // 128):
        ids = jnp.broadcast_to(ids_ref[at : at + 1, :], (height, 128)).astype(jnp.int16)
        parts.append(jnp.where(ids == rows, one, zero))
    return jnp.concatenate(parts, axis=1)


def finish_edges(pre, edges, w_out, gain):
    hidden = silu(pre).astype(BF)
    projected = dot(hidden, w_out)
    return (edges.astype(F32) + layer_norm(projected) * gain).astype(BF)


def pick_kernel(node_ref, border_ref, low_ref, high_ref):
    hot = one_hot(column_of(border_ref, 0, 2 * BORDER), NODES)
    picked = dot(hot, node_ref[...]).astype(BF)
    low_ref[...] = picked[:BORDER]
    high_ref[...] = picked[BORDER:]


def project_kernel(node_ref, w_ref, out_ref):
    nodes = node_ref[...]
    out_ref[:NODES] = dot(nodes, w_ref[2 * D :]).astype(BF)
    out_ref[NODES:] = dot(nodes, w_ref[D : 2 * D]).astype(BF)


def fine_kernel(
    first_row, edge_ref, send_ref, recv_ref, table_ref, low_ref, high_ref, w_in_ref, w_out_ref,
    gain_ref, *rest,
):
    if first_row:
        before_ref, _, new_ref, sum_ref, halo_ref, rows_ref, sems = rest
    else:
        new_ref, sum_ref, halo_ref, rows_ref, sems = rest
    halo_ref[:BORDER] = dot(low_ref[...], w_in_ref[D : 2 * D]).astype(BF)
    halo_ref[BORDER:] = dot(high_ref[...], w_in_ref[D : 2 * D]).astype(BF)
    gain = gain_ref[...]
    copies = []
    for at in range(HALF // BLOCK):
        first = first_row + at * BLOCK
        edges = edge_ref[first : first + BLOCK]
        recv_hot = one_hot(column_of(recv_ref, first, BLOCK), NODES)
        send_hot = one_hot(column_of(send_ref, first, BLOCK), NODES + 2 * BORDER)
        pre = dot(edges, w_in_ref[:D])
        pre = pre + dot(recv_hot, table_ref[:NODES])
        pre = pre + dot(send_hot[:, :NODES], table_ref[NODES:])
        pre = pre + dot(send_hot[:, NODES:], halo_ref[...])
        rows_ref[at * BLOCK : (at + 1) * BLOCK] = finish_edges(pre, edges, w_out_ref[...], gain)
        copies.append(
            pltpu.make_async_copy(
                rows_ref.at[pl.ds(at * BLOCK, BLOCK)], new_ref.at[pl.ds(first, BLOCK)], sems.at[at]
            )
        )
        copies[-1].start()
    hot = one_hot_rows(recv_ref, first_row, HALF, NODES)
    sums = dot(hot, rows_ref[...])
    sum_ref[...] = sums + before_ref[...] if first_row else sums
    for copy in copies:
        copy.wait()


def gather_kernel(send_ref, recv_ref, table_ref, send_out, recv_out):
    for first in range(0, EDGES, BLOCK):
        rows = slice(first, first + BLOCK)
        for ids_ref, out_ref in ((send_ref, send_out), (recv_ref, recv_out)):
            hot = one_hot(column_of(ids_ref, first, BLOCK), table_ref.shape[0])
            out_ref[rows] = dot(hot, table_ref[...]).astype(BF)


def coarse_kernel(
    edge_ref, send_ref, recv_ref, slot_ref, table_ref, send_part, recv_part, w_in_ref, w_out_ref,
    gain_ref, new_ref, mine_ref, theirs_ref,
):
    gain = gain_ref[...]
    half = table_ref.shape[0]
    for first in range(0, EDGES, BLOCK):
        rows = slice(first, first + BLOCK)
        edges = edge_ref[rows]
        pre = dot(edges, w_in_ref[:D])
        for ids_ref, part_ref, at in ((send_ref, send_part, 1), (recv_ref, recv_part, 2)):
            hot = one_hot(column_of(ids_ref, first, BLOCK), half, half)
            picked = (dot(hot, table_ref[...]) + part_ref[rows].astype(F32)).astype(BF)
            pre = pre + dot(picked, w_in_ref[at * D : (at + 1) * D])
        new_ref[rows] = finish_edges(pre, edges, w_out_ref[...], gain)
    height = 2 * mine_ref.shape[0]
    sums = dot(one_hot_rows(slot_ref, 0, EDGES, height), new_ref[...])
    mine_ref[...] = sums[: height // 2]
    theirs_ref[...] = sums[height // 2 :].astype(BF)


def node_rows(nodes, incoming, w_in_ref, w_out_ref, gain):
    pre = dot(nodes, w_in_ref[:D]) + dot(incoming, w_in_ref[D:])
    projected = dot(silu(pre).astype(BF), w_out_ref[...])
    return (nodes.astype(F32) + layer_norm(projected) * gain).astype(BF)


def node_kernel(node_ref, sum_ref, w_in_ref, w_out_ref, gain_ref, out_ref, first_ref):
    for first in range(0, NODES, BLOCK):
        rows = slice(first, first + BLOCK)
        out_ref[rows] = node_rows(
            node_ref[rows], sum_ref[rows].astype(BF), w_in_ref, w_out_ref, gain_ref[...]
        )
    first_ref[...] = sum_ref[:TAIL]


def tail_kernel(
    node_ref, sum_ref, mine_ref, theirs_ref, w_in_ref, w_out_ref, gain_ref, _, out_ref, rows_ref,
    sem,
):
    coarse = mine_ref[:COARSE_ROWS] + theirs_ref[...].astype(F32)
    total = sum_ref[...]
    total = jnp.concatenate([total[:COARSE_ROWS] + coarse, total[COARSE_ROWS:]], axis=0)
    rows_ref[...] = node_rows(
        node_ref[:TAIL], total.astype(BF), w_in_ref, w_out_ref, gain_ref[...]
    )
    copy = pltpu.make_async_copy(rows_ref, out_ref.at[pl.ds(0, TAIL)], sem)
    copy.start()
    copy.wait()


def shape(rows, dtype=BF):
    return jax.ShapeDtypeStruct((rows, D), dtype)


VMEM_SPEC = pl.BlockSpec(memory_space=pltpu.VMEM)
ANY_SPEC = pl.BlockSpec(memory_space=pl.ANY)


def call(kernel, outs, flops, *args, name, scratch=(), out_any=(), in_any=(), aliases=None):
    return pl.pallas_call(
        kernel,
        out_shape=outs,
        in_specs=[ANY_SPEC if at in in_any else VMEM_SPEC for at in range(len(args))],
        out_specs=tuple(
            ANY_SPEC if at in out_any else VMEM_SPEC for at in range(len(outs))
        ),
        scratch_shapes=scratch,
        input_output_aliases=aliases or {},
        compiler_params=pltpu.CompilerParams(vmem_limit_bytes=VMEM_LIMIT),
        cost_estimate=pl.CostEstimate(flops=flops, bytes_accessed=4 << 20, transcendentals=0),
        name=name,
    )(*args)


def patch_pairs(move):
    pairs = []
    for x in range(SIDE):
        for y in range(SIDE):
            for core in range(CORES):
                to_x, to_y, to_core = move(x, y, core)
                pairs.append(
                    ((x * SIDE + y) * CORES + core, (to_x * SIDE + to_y) * CORES + to_core)
                )
    return pairs


def even(i, length):
    return i ^ 1


def odd(i, length):
    return ((i + 1) ^ 1) - 1 if i < length - 1 and i > 0 else length - 1 - i


def along_x(pair):
    return patch_pairs(lambda x, y, c: (pair(x, SIDE), y, c))


def along_y(pair):
    return patch_pairs(lambda x, y, c: (x, pair(y, SIDE), c))


def crossed(pair, turn):
    return patch_pairs(
        lambda x, y, c: (pair(x, SIDE), y, c) if c == turn else (x, pair(y, SIDE), c)
    )


SWAP_CORE = patch_pairs(lambda x, y, c: (x, y, c ^ 1))
Z_EVEN = [(i, even(i, GROUPS)) for i in range(GROUPS)]
Z_ODD = [(i, odd(i, GROUPS)) for i in range(GROUPS)]
tie = lambda *arrays: lax.optimization_barrier(arrays)


def ring_offset(other, mine, length, sign):
    step = jnp.where(mine % 2 == 0, sign, -sign)
    return (other - mine) * step & (length - 1)


def place_4(offset):
    return offset ^ (offset >> 1)


def place_8(offset):
    low, mid, high = offset & 1, offset >> 1 & 1, offset >> 2
    return (low ^ high) | high << 1 | (mid ^ high) << 2


def shards(
    node_lat, fine_edge_lat, fine_send, fine_recv, border_rows, coarse_edge_lat, coarse_send,
    coarse_recv, w_edge_in, w_edge_out, edge_gain, w_node_in, w_node_out, node_gain,
):
    group = lax.axis_index("group")
    patch = lax.axis_index("patch")
    my_core, my_y, my_x = patch & 1, patch >> 1 & 3, patch >> 3
    edge_gain = edge_gain[None, :]
    node_gain = node_gain[None, :]
    grid = lambda ids: ids.reshape(-1, 128)
    swap = lambda rows, pairs: lax.ppermute(rows, "patch", pairs)
    join = lambda *rows: jnp.concatenate(rows, axis=0)

    own = node_lat[:COARSE_ROWS]
    picked_from = tie(own, node_lat)[1]
    pair = lax.ppermute(own, "group", Z_EVEN)
    low, high = call(
        pick_kernel, (shape(BORDER), shape(BORDER)), 2 * 256 * 512 * 512, picked_from,
        grid(border_rows), name="pick",
    )
    pair, low, high = tie(pair, low, high)
    near = join(own, pair)
    near, project_from = tie(near, node_lat)
    next_two = lax.ppermute(near, "group", Z_ODD)
    (table,) = call(
        project_kernel, (shape(2 * NODES),), 4 * 512 * 512 * 512, project_from, w_edge_in,
        name="project",
    )
    next_two, table = tie(next_two, table)
    up = [(i, (i + 1) % PATCHES) for i in range(PATCHES)]
    down = [(j, i) for i, j in up]
    next_two, high = tie(next_two, high)
    far_two = lax.ppermute(next_two, "group", Z_EVEN)
    from_low = lax.ppermute(high, "patch", up)
    far_two, low = tie(far_two, low)
    last_two = lax.ppermute(far_two, "group", Z_ODD)
    from_high = lax.ppermute(low, "patch", down)
    block = join(near, next_two, far_two, last_two)

    block = join(block, swap(block, crossed(even, 0)))
    block, from_low, from_high = tie(block, from_low, from_high)
    other = swap(block, crossed(odd, 0))
    fine_args = (
        fine_edge_lat, grid(fine_send), grid(fine_recv), table, from_low, from_high, w_edge_in,
        w_edge_out, edge_gain,
    )
    fine_scratch = [
        pltpu.VMEM((2 * BORDER, D), BF), pltpu.VMEM((HALF, D), BF),
        pltpu.SemaphoreType.DMA((HALF // BLOCK,)),
    ]
    fine_outs = (shape(EDGES), shape(NODES, F32))
    fine_new, fine_sum = call(
        functools.partial(fine_kernel, 0), fine_outs, 2 << 30, *fine_args, name="fine_first",
        scratch=fine_scratch, out_any=(0,),
    )
    other, fine_sum = tie(other, fine_sum)
    block = join(block, other)

    middle = block.shape[0] // 2
    one, two = block[:middle], block[middle:]
    one, two, fine_sum = tie(one, two, fine_sum)
    one_next, two_next = swap(one, crossed(even, 1)), swap(two, crossed(odd, 1))
    fine_new, fine_sum = call(
        functools.partial(fine_kernel, HALF), fine_outs, 2 << 30, *fine_args, fine_sum, fine_new,
        name="fine_second", scratch=fine_scratch, out_any=(0,), in_any=(len(fine_args) + 1,),
        aliases={len(fine_args) + 1: 0},
    )
    one_next, two_next, fine_sum = tie(one_next, two_next, fine_sum)
    one, two = join(one, one_next), join(two, two_next)
    one, two, fine_sum = tie(one, two, fine_sum)
    one_next, two_next = swap(one, crossed(odd, 1)), swap(two, crossed(even, 1))
    node_main, first_sum = call(
        node_kernel, (shape(NODES), shape(TAIL, F32)), 768 << 20, node_lat, fine_sum, w_node_in,
        w_node_out, node_gain, name="node",
    )
    one_next, two_next, first_sum = tie(one_next, two_next, first_sum)
    part = join(one, one_next, two, two_next)
    other_half = swap(part, SWAP_CORE)

    def place(ids):
        row, at = ids & 7, ids >> 3
        core, y, x, z = at & 1, at >> 1 & 3, at >> 3 & 3, at >> 5
        z = place_8(ring_offset(z, group, GROUPS, 1))
        first, mine_first = jnp.where(core == 0, x, y), jnp.where(core == 0, my_x, my_y)
        second, mine_second = jnp.where(core == 0, y, x), jnp.where(core == 0, my_y, my_x)
        first = place_4(ring_offset(first, mine_first, SIDE, 1))
        second = place_4(ring_offset(second, mine_second, SIDE, 1 - (first >> 1) * 2))
        return (
            (core ^ my_core) << 10 | (first >> 1) << 9 | second << 7 | (first & 1) << 6 | z << 3
            | row
        )

    row, at = coarse_recv & 7, coarse_recv >> 3
    slot = (
        (at & 1 ^ my_core) << 7
        | place_4(ring_offset(at >> 3 & 3, my_x, SIDE, 1)) << 5
        | place_4(ring_offset(at >> 1 & 3, my_y, SIDE, 1)) << 3
        | row
    )
    slot = grid(jnp.where(at >> 5 == group, slot, -1))
    send_place, recv_place = grid(place(coarse_send)), grid(place(coarse_recv))

    send_part, recv_part = call(
        gather_kernel, (shape(EDGES), shape(EDGES)), 2 << 30, send_place, recv_place, part,
        name="gather",
    )
    coarse_new, total, theirs = call(
        coarse_kernel, (shape(EDGES), shape(128, F32), shape(128)), 4 << 30, coarse_edge_lat,
        send_place, recv_place, slot, other_half, send_part, recv_part, w_edge_in, w_edge_out,
        edge_gain, name="coarse",
    )

    total = total + swap(theirs, SWAP_CORE).astype(F32)
    for pairs in (along_x(odd), along_x(even), along_y(odd)):
        width = total.shape[0] // 2
        total = total[:width] + swap(total[width:].astype(BF), pairs).astype(F32)
    theirs = swap(total[COARSE_ROWS:].astype(BF), along_y(even))
    (node_new,) = call(
        tail_kernel, (shape(NODES),), 24 << 20, node_lat, first_sum, total, theirs, w_node_in,
        w_node_out, node_gain, node_main, name="tail",
        scratch=[pltpu.VMEM((TAIL, D), BF), pltpu.SemaphoreType.DMA], out_any=(0,), in_any=(7,),
        aliases={7: 0},
    )
    return (node_new, fine_new, coarse_new)


def solution(mesh):
    in_specs = (
        P(("group", "patch"), None), P(("group", "patch"), None), P(("group", "patch")),
        P(("group", "patch")), P(("group", "patch")), P("patch", None), P("patch"), P("patch"),
        P(), P(), P(), P(), P(), P(),
    )
    out_specs = (P(("group", "patch"), None), P(("group", "patch"), None), P("patch", None))
    return jax.shard_map(shards, mesh=mesh, in_specs=in_specs, out_specs=out_specs, check_vma=False)
```

```python
import functools

import jax
import jax.numpy as jnp
from jax import lax
from jax.experimental import pallas as pl
from jax.experimental.pallas import tpu as pltpu
from jax.sharding import PartitionSpec as P

D = 512
GROUPS = 8
SIDE = 4
CORES = 2
PATCHES = SIDE * SIDE * CORES
BORDER = 128
COARSE_ROWS = 8
EDGES = 1024
NODES = 512
TAIL = 16
EPS = 1e-05
BF = jnp.bfloat16
F32 = jnp.float32
BLOCK = 256
VMEM_LIMIT = 24 * 1024 * 1024


def dot(a, b):
    return jnp.dot(a, b, preferred_element_type=F32)


def silu(values):
    half = 0.5 * values
    return half * jnp.tanh(half) + half


def layer_norm(values):
    average = jnp.mean(values, axis=-1, keepdims=True)
    centred = values - average
    variance = jnp.mean(centred * centred, axis=-1, keepdims=True)
    return centred * lax.rsqrt(variance + EPS)


def column_of(ids_ref, first, rows):
    tiles = []
    for at in range(first // 128, (first + rows) // 128):
        row = jnp.broadcast_to(ids_ref[at : at + 1, :], (128, 128))
        tiles.append(row.T)
    return jnp.concatenate(tiles, axis=0).astype(jnp.int16)


def one_hot(column, width, offset=0):
    lanes = lax.broadcasted_iota(jnp.int16, column.shape, 1)
    one, zero = jnp.ones(column.shape, BF), jnp.zeros(column.shape, BF)
    return jnp.concatenate(
        [
            jnp.where(column == lanes + jnp.int16(offset + 128 * at), one, zero)
            for at in range(width // 128)
        ],
        axis=1,
    )


def one_hot_rows(ids_ref, count, height):
    rows = lax.broadcasted_iota(jnp.int16, (height, 128), 0)
    one, zero = jnp.ones((height, 128), BF), jnp.zeros((height, 128), BF)
    parts = []
    for at in range(count // 128):
        ids = jnp.broadcast_to(ids_ref[at : at + 1, :], (height, 128)).astype(jnp.int16)
        parts.append(jnp.where(ids == rows, one, zero))
    return jnp.concatenate(parts, axis=1)


def send_rows(rows_ref, out_ref, sems, at):
    rows = pl.ds(at * BLOCK, BLOCK)
    copy = pltpu.make_async_copy(rows_ref.at[rows], out_ref.at[rows], sems.at[at])
    copy.start()
    return copy


def load_kernel(*refs):
    count = len(refs) // 2
    sems = refs[-1]
    copies = [
        pltpu.make_async_copy(refs[at], refs[count + at], sems.at[at]) for at in range(count)
    ]
    for copy in copies:
        copy.start()
    for copy in copies:
        copy.wait()


def finish_edges(pre, edges, w_out, gain):
    hidden = silu(pre).astype(BF)
    projected = dot(hidden, w_out)
    return (edges.astype(F32) + layer_norm(projected) * gain).astype(BF)


def pick_kernel(node_ref, border_ref, low_ref, high_ref):
    hot = one_hot(column_of(border_ref, 0, 2 * BORDER), NODES)
    picked = dot(hot, node_ref[...]).astype(BF)
    low_ref[...] = picked[:BORDER]
    high_ref[...] = picked[BORDER:]


def project_kernel(node_ref, w_ref, out_ref):
    nodes = node_ref[...]
    out_ref[:NODES] = dot(nodes, w_ref[2 * D :]).astype(BF)
    out_ref[NODES:] = dot(nodes, w_ref[D : 2 * D]).astype(BF)


def fine_kernel(
    edge_ref, send_ref, recv_ref, table_ref, low_ref, high_ref, w_in_ref, w_out_ref, gain_ref,
    new_ref, sum_ref, halo_ref, rows_ref, sems,
):
    halo_ref[:BORDER] = dot(low_ref[...], w_in_ref[D : 2 * D]).astype(BF)
    halo_ref[BORDER:] = dot(high_ref[...], w_in_ref[D : 2 * D]).astype(BF)
    gain = gain_ref[...]
    copies = []
    for at in range(EDGES // BLOCK):
        first = at * BLOCK
        edges = edge_ref[first : first + BLOCK]
        recv_hot = one_hot(column_of(recv_ref, first, BLOCK), NODES)
        send_hot = one_hot(column_of(send_ref, first, BLOCK), NODES + 2 * BORDER)
        pre = dot(edges, w_in_ref[:D])
        pre = pre + dot(recv_hot, table_ref[:NODES])
        pre = pre + dot(send_hot[:, :NODES], table_ref[NODES:])
        pre = pre + dot(send_hot[:, NODES:], halo_ref[...])
        rows_ref[first : first + BLOCK] = finish_edges(pre, edges, w_out_ref[...], gain)
        copies.append(send_rows(rows_ref, new_ref, sems, at))
    sum_ref[...] = dot(one_hot_rows(recv_ref, EDGES, NODES), rows_ref[...])
    for copy in copies:
        copy.wait()


def gather_kernel(send_ref, recv_ref, table_ref, send_out, recv_out):
    for first in range(0, EDGES, BLOCK):
        rows = slice(first, first + BLOCK)
        for ids_ref, out_ref in ((send_ref, send_out), (recv_ref, recv_out)):
            hot = one_hot(column_of(ids_ref, first, BLOCK), table_ref.shape[0])
            out_ref[rows] = dot(hot, table_ref[...]).astype(BF)


def coarse_kernel(
    edge_ref, send_ref, recv_ref, slot_ref, table_ref, send_part, recv_part, w_in_ref, w_out_ref,
    gain_ref, new_ref, sum_ref, rows_ref, sems,
):
    gain = gain_ref[...]
    half = table_ref.shape[0]
    copies = []
    for at in range(EDGES // BLOCK):
        first = at * BLOCK
        rows = slice(first, first + BLOCK)
        edges = edge_ref[rows]
        pre = dot(edges, w_in_ref[:D])
        for ids_ref, part_ref, part in ((send_ref, send_part, 1), (recv_ref, recv_part, 2)):
            hot = one_hot(column_of(ids_ref, first, BLOCK), half, half)
            picked = (dot(hot, table_ref[...]) + part_ref[rows].astype(F32)).astype(BF)
            pre = pre + dot(picked, w_in_ref[part * D : (part + 1) * D])
        rows_ref[rows] = finish_edges(pre, edges, w_out_ref[...], gain)
        copies.append(send_rows(rows_ref, new_ref, sems, at))
    sum_ref[...] = dot(one_hot_rows(slot_ref, EDGES, sum_ref.shape[0]), rows_ref[...]).astype(BF)
    for copy in copies:
        copy.wait()


def node_rows(nodes, incoming, w_in_ref, w_out_ref, gain):
    pre = dot(nodes, w_in_ref[:D]) + dot(incoming, w_in_ref[D:])
    projected = dot(silu(pre).astype(BF), w_out_ref[...])
    return (nodes.astype(F32) + layer_norm(projected) * gain).astype(BF)


def node_kernel(node_ref, sum_ref, w_in_ref, w_out_ref, gain_ref, out_ref, first_ref):
    for first in range(0, NODES, BLOCK):
        rows = slice(first, first + BLOCK)
        out_ref[rows] = node_rows(
            node_ref[rows], sum_ref[rows].astype(BF), w_in_ref, w_out_ref, gain_ref[...]
        )
    first_ref[...] = sum_ref[:TAIL]


def tail_kernel(
    node_ref, sum_ref, parts_ref, w_in_ref, w_out_ref, gain_ref, _, out_ref, rows_ref, sem
):
    parts = parts_ref[...].astype(F32).reshape(PATCHES, COARSE_ROWS, D)
    total = sum_ref[...]
    total = jnp.concatenate(
        [total[:COARSE_ROWS] + jnp.sum(parts, axis=0), total[COARSE_ROWS:]], axis=0
    )
    rows_ref[...] = node_rows(
        node_ref[:TAIL], total.astype(BF), w_in_ref, w_out_ref, gain_ref[...]
    )
    copy = pltpu.make_async_copy(rows_ref, out_ref.at[pl.ds(0, TAIL)], sem)
    copy.start()
    copy.wait()


def shape(rows, dtype=BF):
    return jax.ShapeDtypeStruct((rows, D), dtype)


VMEM_SPEC = pl.BlockSpec(memory_space=pltpu.VMEM)
ANY_SPEC = pl.BlockSpec(memory_space=pl.ANY)
HBM_SPEC = pl.BlockSpec(memory_space=pltpu.HBM)


def call(
    kernel, outs, flops, *args, name, scratch=(), out_any=(), in_any=(), aliases=None, spec=ANY_SPEC
):
    return pl.pallas_call(
        kernel,
        out_shape=outs,
        in_specs=[spec if at in in_any else VMEM_SPEC for at in range(len(args))],
        out_specs=tuple(
            ANY_SPEC if at in out_any else VMEM_SPEC for at in range(len(outs))
        ),
        scratch_shapes=scratch,
        input_output_aliases=aliases or {},
        compiler_params=pltpu.CompilerParams(vmem_limit_bytes=VMEM_LIMIT),
        cost_estimate=pl.CostEstimate(flops=flops, bytes_accessed=4 << 20, transcendentals=0),
        name=name,
    )(*args)


def patch_pairs(move):
    pairs = []
    for x in range(SIDE):
        for y in range(SIDE):
            for core in range(CORES):
                to_x, to_y, to_core = move(x, y, core)
                pairs.append(
                    ((x * SIDE + y) * CORES + core, (to_x * SIDE + to_y) * CORES + to_core)
                )
    return pairs


def even(i, length):
    return i ^ 1


def odd(i, length):
    return ((i + 1) ^ 1) - 1 if i < length - 1 and i > 0 else length - 1 - i


def crossed(k, turn):
    return patch_pairs(lambda x, y, c: (x ^ k, y, c) if c == turn else (x, y ^ k, c))


SWAP_CORE = patch_pairs(lambda x, y, c: (x, y, c ^ 1))
Z_EVEN = [(i, even(i, GROUPS)) for i in range(GROUPS)]
Z_ODD = [(i, odd(i, GROUPS)) for i in range(GROUPS)]
tie = lambda *arrays: lax.optimization_barrier(arrays)


def ring_offset(other, mine, length):
    step = jnp.where(mine & 1 == 0, 1, -1)
    return (other - mine) * step & (length - 1)


def place_8(offset):
    low, mid, high = offset & 1, offset >> 1 & 1, offset >> 2
    return (low ^ high) | high << 1 | (mid ^ high) << 2


def shards(
    node_lat, fine_edge_lat, fine_send, fine_recv, border_rows, coarse_edge_lat, coarse_send,
    coarse_recv, w_edge_in, w_edge_out, edge_gain, w_node_in, w_node_out, node_gain,
):
    group = lax.axis_index("group")
    patch = lax.axis_index("patch")
    my_core, my_y, my_x = patch & 1, patch >> 1 & 3, patch >> 3
    edge_gain = edge_gain[None, :]
    node_gain = node_gain[None, :]
    grid = lambda ids: ids.reshape(-1, 128)
    swap = lambda rows, pairs: lax.ppermute(rows, "patch", pairs)
    join = lambda *rows: jnp.concatenate(rows, axis=0)

    def place(ids):
        row, at = ids & 7, ids >> 3
        core, y, x, z = at & 1, (at >> 1 & 3) ^ my_y, (at >> 3 & 3) ^ my_x, at >> 5
        first, second = jnp.where(core == 0, x, y), jnp.where(core == 0, y, x)
        return (
            (core ^ my_core) << 10 | second << 8 | first << 6
            | place_8(ring_offset(z, group, GROUPS)) << 3 | row
        )

    send_place, recv_place = grid(place(coarse_send)), grid(place(coarse_recv))
    slot = grid(jnp.where(coarse_recv >> 8 == group, coarse_recv & 255, -1))

    def load(name, *arrays):
        return call(
            load_kernel, [jax.ShapeDtypeStruct(a.shape, a.dtype) for a in arrays], 0,
            *[pltpu.with_memory_space_constraint(a, pltpu.HBM) for a in arrays],
            name=name, scratch=[pltpu.SemaphoreType.DMA((len(arrays),))],
            in_any=range(len(arrays)), spec=HBM_SPEC,
        )

    own = node_lat[:COARSE_ROWS]
    own, *loads = tie(own, node_lat, w_edge_in, w_edge_out, border_rows)
    pair = lax.ppermute(own, "group", Z_EVEN)
    nodes, w_in, w_out = load("load_first", *loads[:3])
    pair, nodes, w_in, w_out = tie(pair, nodes, w_in, w_out)
    near = join(own, pair)
    near, nodes, *loads = tie(
        near, nodes, fine_edge_lat, coarse_edge_lat, w_node_in, w_node_out
    )
    next_two = lax.ppermute(near, "group", Z_ODD)
    low, high = call(
        pick_kernel, (shape(BORDER), shape(BORDER)), 2 * 256 * 512 * 512, nodes,
        grid(border_rows), name="pick",
    )
    fine_edges, coarse_edges, w_node, w_node_last = load("load_second", *loads)
    next_two, low, high, fine_edges, coarse_edges, w_node, w_node_last = tie(
        next_two, low, high, fine_edges, coarse_edges, w_node, w_node_last
    )
    up = [(i, (i + 1) % PATCHES) for i in range(PATCHES)]
    down = [(j, i) for i, j in up]
    far_two = lax.ppermute(next_two, "group", Z_EVEN)
    from_low = lax.ppermute(high, "patch", up)
    far_two, low = tie(far_two, low)
    last_two = lax.ppermute(far_two, "group", Z_ODD)
    from_high = lax.ppermute(low, "patch", down)
    block = join(near, next_two, far_two, last_two)

    block, nodes, w_in = tie(block, nodes, w_in)
    others = [swap(block, crossed(k, 0)) for k in (1, 2, 3)]
    (table,) = call(
        project_kernel, (shape(2 * NODES),), 4 * 512 * 512 * 512, nodes, w_in, name="project"
    )
    *others, table, from_low, from_high = tie(*others, table, from_low, from_high)
    block = join(block, *others)

    block, table = tie(block, table)
    others = [swap(block, crossed(k, 1)) for k in (1, 2, 3)]
    fine_new, fine_sum = call(
        fine_kernel, (shape(EDGES), shape(NODES, F32)), 4 << 30, fine_edges, grid(fine_send),
        grid(fine_recv), table, from_low, from_high, w_in, w_out, edge_gain, name="fine",
        scratch=[
            pltpu.VMEM((2 * BORDER, D), BF), pltpu.VMEM((EDGES, D), BF),
            pltpu.SemaphoreType.DMA((EDGES // BLOCK,)),
        ], out_any=(0,),
    )
    node_main, first_sum = call(
        node_kernel, (shape(NODES), shape(TAIL, F32)), 768 << 20, nodes, fine_sum, w_node,
        w_node_last, node_gain, name="node",
    )
    *others, first_sum = tie(*others, first_sum)
    part = join(block, *others)
    other_half = swap(part, SWAP_CORE)

    send_part, recv_part = call(
        gather_kernel, (shape(EDGES), shape(EDGES)), 2 << 30, send_place, recv_place, part,
        name="gather",
    )
    coarse_new, sums = call(
        coarse_kernel, (shape(EDGES), shape(PATCHES * COARSE_ROWS)), 4 << 30, coarse_edges,
        send_place, recv_place, slot, other_half, send_part, recv_part, w_in, w_out, edge_gain,
        name="coarse",
        scratch=[pltpu.VMEM((EDGES, D), BF), pltpu.SemaphoreType.DMA((EDGES // BLOCK,))],
        out_any=(0,),
    )

    parts = lax.all_to_all(sums.reshape(PATCHES, COARSE_ROWS, D), "patch", 0, 0)
    (node_new,) = call(
        tail_kernel, (shape(NODES),), 24 << 20, nodes, first_sum, parts.reshape(-1, D), w_node,
        w_node_last, node_gain, node_main, name="tail",
        scratch=[pltpu.VMEM((TAIL, D), BF), pltpu.SemaphoreType.DMA], out_any=(0,), in_any=(6,),
        aliases={6: 0},
    )
    return (node_new, fine_new, coarse_new)


def solution(mesh):
    in_specs = (
        P(("group", "patch"), None), P(("group", "patch"), None), P(("group", "patch")),
        P(("group", "patch")), P(("group", "patch")), P("patch", None), P("patch"), P("patch"),
        P(), P(), P(), P(), P(), P(),
    )
    out_specs = (P(("group", "patch"), None), P(("group", "patch"), None), P("patch", None))
    return jax.shard_map(shards, mesh=mesh, in_specs=in_specs, out_specs=out_specs, check_vma=False)
```

```python
import functools

import jax
import jax.numpy as jnp
from jax import lax
from jax.experimental import pallas as pl
from jax.experimental.pallas import tpu as pltpu
from jax.sharding import PartitionSpec as P

D = 512
GROUPS = 8
SIDE = 4
CORES = 2
PATCHES = SIDE * SIDE * CORES
BORDER = 128
COARSE_ROWS = 8
EDGES = 1024
NODES = 512
TAIL = 16
EPS = 1e-05
BF = jnp.bfloat16
F32 = jnp.float32
BLOCK = 512
VMEM_LIMIT = 24 * 1024 * 1024


def dot(a, b):
    return jnp.dot(a, b, preferred_element_type=F32)


def silu(values):
    half = 0.5 * values
    return half * jnp.tanh(half) + half


def layer_norm(values):
    average = jnp.mean(values, axis=-1, keepdims=True)
    centred = values - average
    variance = jnp.mean(centred * centred, axis=-1, keepdims=True)
    return centred * lax.rsqrt(variance + EPS)


def column_of(ids_ref, first, rows):
    tiles = []
    for at in range(first // 128, (first + rows) // 128):
        row = jnp.broadcast_to(ids_ref[at : at + 1, :], (128, 128))
        tiles.append(row.T)
    return jnp.concatenate(tiles, axis=0).astype(jnp.int16)


def one_hot(column, width, offset=0):
    lanes = lax.broadcasted_iota(jnp.int16, column.shape, 1)
    one, zero = jnp.ones(column.shape, BF), jnp.zeros(column.shape, BF)
    return jnp.concatenate(
        [
            jnp.where(column == lanes + jnp.int16(offset + 128 * at), one, zero)
            for at in range(width // 128)
        ],
        axis=1,
    )


def one_hot_rows(ids_ref, count, height):
    rows = lax.broadcasted_iota(jnp.int16, (height, 128), 0)
    one, zero = jnp.ones((height, 128), BF), jnp.zeros((height, 128), BF)
    parts = []
    for at in range(count // 128):
        ids = jnp.broadcast_to(ids_ref[at : at + 1, :], (height, 128)).astype(jnp.int16)
        parts.append(jnp.where(ids == rows, one, zero))
    return jnp.concatenate(parts, axis=1)


def send_rows(rows_ref, out_ref, sems, at):
    rows = pl.ds(at * BLOCK, BLOCK)
    copy = pltpu.make_async_copy(rows_ref.at[rows], out_ref.at[rows], sems.at[at])
    copy.start()
    return copy


def load_kernel(*refs):
    count = len(refs) // 2
    sems = refs[-1]
    copies = [
        pltpu.make_async_copy(refs[at], refs[count + at], sems.at[at]) for at in range(count)
    ]
    for copy in copies:
        copy.start()
    for copy in copies:
        copy.wait()


def finish_edges(pre, edges, w_out, gain):
    hidden = silu(pre).astype(BF)
    projected = dot(hidden, w_out)
    return (edges.astype(F32) + layer_norm(projected) * gain).astype(BF)


def pick_kernel(
    border_ref, node_in, w_in, w_out, inner_ref, outer_ref, node_ref, w_in_ref, w_out_ref, sems
):
    copies = [
        pltpu.make_async_copy(source, target, sems.at[at])
        for at, (source, target) in enumerate(
            ((node_in, node_ref), (w_in, w_in_ref), (w_out, w_out_ref))
        )
    ]
    for copy in copies:
        copy.start()
    hot = one_hot(column_of(border_ref, 0, 2 * BORDER), NODES)
    copies[0].wait()
    picked = dot(hot, node_ref[...]).astype(BF)
    inner_ref[...] = picked[:BORDER]
    outer_ref[...] = picked[BORDER:]
    for copy in copies[1:]:
        copy.wait()


def project_kernel(node_ref, w_ref, out_ref):
    nodes = node_ref[...]
    out_ref[:NODES] = dot(nodes, w_ref[2 * D :]).astype(BF)
    out_ref[NODES:] = dot(nodes, w_ref[D : 2 * D]).astype(BF)


def fine_kernel(
    edge_ref, send_ref, recv_ref, table_ref, inner_ref, outer_ref, w_in_ref, w_out_ref, gain_ref,
    new_ref, sum_ref, halo_ref, rows_ref, sem,
):
    halo_ref[:BORDER] = dot(inner_ref[...], w_in_ref[D : 2 * D]).astype(BF)
    halo_ref[BORDER:] = dot(outer_ref[...], w_in_ref[D : 2 * D]).astype(BF)
    edges = edge_ref[...]
    recv_hot = one_hot(column_of(recv_ref, 0, EDGES), NODES)
    send_hot = one_hot(column_of(send_ref, 0, EDGES), NODES + 2 * BORDER)
    pre = dot(edges, w_in_ref[:D])
    pre = pre + dot(jnp.concatenate([recv_hot, send_hot[:, :NODES]], axis=1), table_ref[...])
    pre = pre + dot(send_hot[:, NODES:], halo_ref[...])
    rows_ref[...] = finish_edges(pre, edges, w_out_ref[...], gain_ref[...])
    copy = pltpu.make_async_copy(rows_ref, new_ref, sem)
    copy.start()
    sum_ref[...] = dot(one_hot_rows(recv_ref, EDGES, NODES), rows_ref[...])
    copy.wait()


def gather_kernel(send_ref, recv_ref, table_ref, send_out, recv_out):
    for first in range(0, EDGES, BLOCK):
        rows = slice(first, first + BLOCK)
        for ids_ref, out_ref in ((send_ref, send_out), (recv_ref, recv_out)):
            hot = one_hot(column_of(ids_ref, first, BLOCK), table_ref.shape[0])
            out_ref[rows] = dot(hot, table_ref[...]).astype(BF)


def coarse_kernel(
    edge_ref, send_ref, recv_ref, slot_ref, table_ref, send_part, recv_part, w_in_ref, w_out_ref,
    gain_ref, new_ref, mine_ref, theirs_ref, rows_ref, sems,
):
    gain = gain_ref[...]
    half = table_ref.shape[0]
    copies = []
    for at in range(EDGES // BLOCK):
        rows = slice(at * BLOCK, (at + 1) * BLOCK)
        edges = edge_ref[rows]
        joined = [edges]
        for ids_ref, part_ref in ((send_ref, send_part), (recv_ref, recv_part)):
            hot = one_hot(column_of(ids_ref, at * BLOCK, BLOCK), half, half)
            joined.append((dot(hot, table_ref[...]) + part_ref[rows].astype(F32)).astype(BF))
        pre = dot(jnp.concatenate(joined, axis=1), w_in_ref[...])
        rows_ref[rows] = finish_edges(pre, edges, w_out_ref[...], gain)
        copies.append(send_rows(rows_ref, new_ref, sems, at))
    sums = dot(one_hot_rows(slot_ref, EDGES, 2 * mine_ref.shape[0]), rows_ref[...])
    mine_ref[...] = sums[: mine_ref.shape[0]]
    theirs_ref[...] = sums[mine_ref.shape[0] :].astype(BF)
    for copy in copies:
        copy.wait()


def finish_nodes(pre, nodes, w_out_ref, gain):
    projected = dot(silu(pre).astype(BF), w_out_ref[...])
    return (nodes.astype(F32) + layer_norm(projected) * gain).astype(BF)


def node_kernel(node_ref, sum_ref, w_in_ref, w_out_ref, gain_ref, out_ref, first_ref, pre_ref):
    nodes = node_ref[...]
    pre = dot(nodes, w_in_ref[:D])
    pre_ref[...] = pre[:TAIL]
    first_ref[...] = sum_ref[:TAIL]
    pre = pre + dot(sum_ref[...].astype(BF), w_in_ref[D:])
    out_ref[...] = finish_nodes(pre, nodes, w_out_ref, gain_ref[...])


def tail_kernel(
    node_ref, sum_ref, pre_ref, parts_ref, w_in_ref, w_out_ref, gain_ref, _, out_ref, rows_ref, sem
):
    parts = parts_ref[...].astype(F32).reshape(-1, COARSE_ROWS, D)
    total = sum_ref[...]
    total = jnp.concatenate(
        [total[:COARSE_ROWS] + jnp.sum(parts, axis=0), total[COARSE_ROWS:]], axis=0
    )
    pre = pre_ref[...] + dot(total.astype(BF), w_in_ref[D:])
    rows_ref[...] = finish_nodes(pre, node_ref[:TAIL], w_out_ref, gain_ref[...])
    copy = pltpu.make_async_copy(rows_ref, out_ref.at[pl.ds(0, TAIL)], sem)
    copy.start()
    copy.wait()


def shape(rows, dtype=BF):
    return jax.ShapeDtypeStruct((rows, D), dtype)


VMEM_SPEC = pl.BlockSpec(memory_space=pltpu.VMEM)
ANY_SPEC = pl.BlockSpec(memory_space=pl.ANY)
HBM_SPEC = pl.BlockSpec(memory_space=pltpu.HBM)


def call(
    kernel, outs, flops, *args, name, scratch=(), out_any=(), in_any=(), aliases=None, spec=ANY_SPEC
):
    return pl.pallas_call(
        kernel,
        out_shape=outs,
        in_specs=[spec if at in in_any else VMEM_SPEC for at in range(len(args))],
        out_specs=tuple(
            ANY_SPEC if at in out_any else VMEM_SPEC for at in range(len(outs))
        ),
        scratch_shapes=scratch,
        input_output_aliases=aliases or {},
        compiler_params=pltpu.CompilerParams(vmem_limit_bytes=VMEM_LIMIT),
        cost_estimate=pl.CostEstimate(flops=flops, bytes_accessed=4 << 20, transcendentals=0),
        name=name,
    )(*args)


def patch_pairs(move):
    pairs = []
    for x in range(SIDE):
        for y in range(SIDE):
            for core in range(CORES):
                to_x, to_y, to_core = move(x, y, core)
                pairs.append(
                    ((x * SIDE + y) * CORES + core, (to_x * SIDE + to_y) * CORES + to_core)
                )
    return pairs


def crossed(k, turn):
    return patch_pairs(lambda x, y, c: (x ^ k, y, c) if c == turn else (x, y ^ k, c))


SWAP_CORE = patch_pairs(lambda x, y, c: (x, y, c ^ 1))


def along_z(move):
    pairs = []
    for group in range(GROUPS):
        pair, member = move(group >> 1, group & 1)
        target = ((pair % (GROUPS // 2)) << 1 | member) * PATCHES
        pairs += [(group * PATCHES + i, target + (i ^ 1)) for i in range(PATCHES)]
    return pairs


Z_PAIR = along_z(lambda pair, member: (pair, member ^ 1))
Z_FAR = along_z(lambda pair, member: (pair + 2, member ^ 1))
Z_MID = along_z(lambda pair, member: (pair - 1 + 2 * member, member))
Z_NEAR = along_z(lambda pair, member: (pair - 1 + 2 * member, member ^ 1))
OUTER = [(i, (i + 1 if i & 1 else i - 1) % PATCHES) for i in range(PATCHES)]
SAME_CORE = [[2 * i + core for i in range(PATCHES // 2)] for core in range(CORES)]
tie = lambda *arrays: lax.optimization_barrier(arrays)


def place_z(group, mine):
    away = ((group >> 1) - (mine >> 1)) * jnp.where(mine & 1 == 0, 1, -1) & 3
    high = away >> 1
    place = ((away ^ high) & 1) << 2 | high << 1 | ((group ^ mine) & 1 ^ high)
    return place, (place & 1) ^ jnp.where(place >= 2, 1, 0)


def shards(
    node_lat, fine_edge_lat, fine_send, fine_recv, border_rows, coarse_edge_lat, coarse_send,
    coarse_recv, w_edge_in, w_edge_out, edge_gain, w_node_in, w_node_out, node_gain,
):
    group = lax.axis_index("group")
    patch = lax.axis_index("patch")
    my_core, my_y, my_x = patch & 1, patch >> 1 & 3, patch >> 3
    edge_gain = edge_gain[None, :]
    node_gain = node_gain[None, :]
    grid = lambda ids: ids.reshape(-1, 128)
    swap = lambda rows, pairs: lax.ppermute(rows, "patch", pairs)
    join = lambda *rows: jnp.concatenate(rows, axis=0)

    turn = lambda away: away ^ (away >> 1)

    def place(ids):
        row, at = ids & 7, ids >> 3
        core, y, x = at & 1, turn(at >> 1 & 3 ^ my_y), turn(at >> 3 & 3 ^ my_x)
        z, exchanged = place_z(at >> 5, group)
        half = core ^ my_core ^ exchanged
        x_first = half == my_core
        first, second = jnp.where(x_first, x, y), jnp.where(x_first, y, x)
        return half << 10 | second << 8 | first << 6 | z << 3 | row

    send_place, recv_place = grid(place(coarse_send)), grid(place(coarse_recv))
    slot = (coarse_recv >> 3 & 1 ^ my_core) << 7 | (coarse_recv >> 4 & 15) << 3 | coarse_recv & 7
    slot = grid(jnp.where(coarse_recv >> 8 == group, slot, -1))
    lower, upper = border_rows[:BORDER], border_rows[BORDER:]
    borders = jnp.stack(
        [jnp.where(my_core == 0, upper, lower), jnp.where(my_core == 0, lower, upper)]
    )
    fine_place = grid(
        jnp.where((fine_send >= NODES) & (my_core == 0), fine_send ^ BORDER, fine_send)
    )
    in_hbm = lambda *arrays: [pltpu.with_memory_space_constraint(a, pltpu.HBM) for a in arrays]
    like = lambda *arrays: [jax.ShapeDtypeStruct(a.shape, a.dtype) for a in arrays]

    own = node_lat[:COARSE_ROWS]
    own, *loads = tie(own, node_lat, w_edge_in, w_edge_out)
    pair = lax.ppermute(own, ("group", "patch"), Z_PAIR)
    inner, outer, nodes, w_in, w_out = call(
        pick_kernel, [shape(BORDER), shape(BORDER), *like(*loads)], 2 * 256 * 512 * 512, borders,
        *in_hbm(*loads), name="pick", scratch=[pltpu.SemaphoreType.DMA((3,))], in_any=(1, 2, 3),
        spec=HBM_SPEC,
    )
    pair, inner, outer, nodes, w_in, w_out = tie(pair, inner, outer, nodes, w_in, w_out)
    near = join(own, pair)
    near, inner, outer = tie(near, inner, outer)
    others = [lax.ppermute(near, ("group", "patch"), to) for to in (Z_NEAR, Z_MID, Z_FAR)]
    inner, outer = swap(inner, SWAP_CORE), swap(outer, OUTER)
    block = join(near, *others)

    block, nodes, w_in, *loads = tie(
        block, nodes, w_in, fine_edge_lat, coarse_edge_lat, w_node_in, w_node_out
    )
    others = [swap(block, crossed(k, 0)) for k in (1, 3, 2)]
    (table,) = call(
        project_kernel, (shape(2 * NODES),), 4 * 512 * 512 * 512, nodes, w_in, name="project"
    )
    fine_edges, coarse_edges, w_node, w_node_last = call(
        load_kernel, like(*loads), 0, *in_hbm(*loads), name="load",
        scratch=[pltpu.SemaphoreType.DMA((len(loads),))], in_any=range(len(loads)), spec=HBM_SPEC,
    )
    *others, table, inner, outer, fine_edges, coarse_edges, w_node, w_node_last = tie(
        *others, table, inner, outer, fine_edges, coarse_edges, w_node, w_node_last
    )
    block = join(block, *others)

    block, table = tie(block, table)
    others = [swap(block, crossed(k, 1)) for k in (1, 3, 2)]
    fine_new, fine_sum = call(
        fine_kernel, (shape(EDGES), shape(NODES, F32)), 4 << 30, fine_edges, fine_place,
        grid(fine_recv), table, inner, outer, w_in, w_out, edge_gain, name="fine",
        scratch=[
            pltpu.VMEM((2 * BORDER, D), BF), pltpu.VMEM((EDGES, D), BF), pltpu.SemaphoreType.DMA
        ], out_any=(0,),
    )
    node_main, first_sum, first_pre = call(
        node_kernel, (shape(NODES), shape(TAIL, F32), shape(TAIL, F32)), 768 << 20, nodes,
        fine_sum, w_node, w_node_last, node_gain, name="node",
    )
    *others, first_sum = tie(*others, first_sum)
    part = join(block, *others)
    other_half = swap(part, SWAP_CORE)

    send_part, recv_part = call(
        gather_kernel, (shape(EDGES), shape(EDGES)), 2 << 30, send_place, recv_place, part,
        name="gather",
    )
    coarse_new, mine, theirs = call(
        coarse_kernel, (shape(EDGES), shape(128, F32), shape(128)), 4 << 30, coarse_edges,
        send_place, recv_place, slot, other_half, send_part, recv_part, w_in, w_out, edge_gain,
        name="coarse",
        scratch=[pltpu.VMEM((EDGES, D), BF), pltpu.SemaphoreType.DMA((EDGES // BLOCK,))],
        out_any=(0,),
    )

    sums = (mine + swap(theirs, SWAP_CORE).astype(F32)).astype(BF)
    parts = lax.all_to_all(
        sums.reshape(-1, COARSE_ROWS, D), "patch", 0, 0, axis_index_groups=SAME_CORE
    )
    (node_new,) = call(
        tail_kernel, (shape(NODES),), 24 << 20, nodes, first_sum, first_pre, parts.reshape(-1, D),
        w_node, w_node_last, node_gain, node_main, name="tail",
        scratch=[pltpu.VMEM((TAIL, D), BF), pltpu.SemaphoreType.DMA], out_any=(0,), in_any=(7,),
        aliases={7: 0},
    )
    return (node_new, fine_new, coarse_new)


def solution(mesh):
    in_specs = (
        P(("group", "patch"), None), P(("group", "patch"), None), P(("group", "patch")),
        P(("group", "patch")), P(("group", "patch")), P("patch", None), P("patch"), P("patch"),
        P(), P(), P(), P(), P(), P(),
    )
    out_specs = (P(("group", "patch"), None), P(("group", "patch"), None), P("patch", None))
    return jax.shard_map(shards, mesh=mesh, in_specs=in_specs, out_specs=out_specs, check_vma=False)
```

```python
import functools

import jax
import jax.numpy as jnp
from jax import lax
from jax.experimental import pallas as pl
from jax.experimental.pallas import tpu as pltpu
from jax.sharding import PartitionSpec as P

D = 512
GROUPS = 8
SIDE = 4
CORES = 2
PATCHES = SIDE * SIDE * CORES
BORDER = 128
COARSE_ROWS = 8
EDGES = 1024
HALF = 512
NODES = 512
TAIL = 16
EPS = 1e-05
BF = jnp.bfloat16
F32 = jnp.float32
BLOCK = 512
VMEM_LIMIT = 10 * 1024 * 1024


def dot(a, b):
    return jnp.dot(a, b, preferred_element_type=F32)


def silu(values):
    half = 0.5 * values
    return half * jnp.tanh(half) + half


def layer_norm(values):
    average = jnp.mean(values, axis=-1, keepdims=True)
    centred = values - average
    variance = jnp.mean(centred * centred, axis=-1, keepdims=True)
    return centred * lax.rsqrt(variance + EPS)


def column_of(ids_ref, first, rows):
    tiles = []
    for at in range(first // 128, (first + rows) // 128):
        row = jnp.broadcast_to(ids_ref[at : at + 1, :], (128, 128))
        tiles.append(row.T)
    return jnp.concatenate(tiles, axis=0).astype(jnp.int16)


def one_hot(column, width, offset=0):
    lanes = lax.broadcasted_iota(jnp.int16, column.shape, 1)
    one, zero = jnp.ones(column.shape, BF), jnp.zeros(column.shape, BF)
    return jnp.concatenate(
        [
            jnp.where(column == lanes + jnp.int16(offset + 128 * at), one, zero)
            for at in range(width // 128)
        ],
        axis=1,
    )


def one_hot_rows(ids_ref, first, count, height):
    rows = lax.broadcasted_iota(jnp.int16, (height, 128), 0)
    one, zero = jnp.ones((height, 128), BF), jnp.zeros((height, 128), BF)
    parts = []
    for at in range(first // 128, (first + count) // 128):
        ids = jnp.broadcast_to(ids_ref[at : at + 1, :], (height, 128)).astype(jnp.int16)
        parts.append(jnp.where(ids == rows, one, zero))
    return jnp.concatenate(parts, axis=1)


def send_rows(rows_ref, out_ref, sems, at):
    rows = pl.ds(at * BLOCK, BLOCK)
    copy = pltpu.make_async_copy(rows_ref.at[rows], out_ref.at[rows], sems.at[at])
    copy.start()
    return copy


def finish_edges(pre, edges, w_out, gain):
    hidden = silu(pre).astype(BF)
    projected = dot(hidden, w_out)
    return (edges.astype(F32) + layer_norm(projected) * gain).astype(BF)


def pick_kernel(
    border_in, node_in, w_in, w_out, inner_ref, outer_ref, node_ref, w_in_ref, w_out_ref,
    border_ref, sems,
):
    copies = [
        pltpu.make_async_copy(source, target, sems.at[at])
        for at, (source, target) in enumerate(
            (
                (border_in, border_ref), (node_in, node_ref), (w_in, w_in_ref),
                (w_out, w_out_ref),
            )
        )
    ]
    for copy in copies:
        copy.start()
    copies[0].wait()
    hot = one_hot(column_of(border_ref, 0, 2 * BORDER), NODES)
    copies[1].wait()
    picked = dot(hot, node_ref[...]).astype(BF)
    lower, upper = picked[:BORDER], picked[BORDER:]
    on_first = lax.axis_index("patch") % CORES == 0
    inner_ref[...] = jnp.where(on_first, upper, lower)
    outer_ref[...] = jnp.where(on_first, lower, upper)
    for copy in copies[2:]:
        copy.wait()


def project_kernel(node_ref, w_ref, out_ref):
    nodes = node_ref[...]
    out_ref[:NODES] = dot(nodes, w_ref[2 * D :]).astype(BF)
    out_ref[NODES:] = dot(nodes, w_ref[D : 2 * D]).astype(BF)


def fine_kernel(
    first, edge_ref, send_ref, recv_ref, table_ref, inner_ref, outer_ref, w_in_ref, w_out_ref,
    gain_ref, *rest,
):
    if first:
        halo_in, before_ref, _, new_ref, sum_ref, rows_ref, sem = rest
        halo = halo_in[...]
    else:
        new_ref, sum_ref, halo_out, rows_ref, sem = rest
        halo_out[:BORDER] = dot(inner_ref[...], w_in_ref[D : 2 * D]).astype(BF)
        halo_out[BORDER:] = dot(outer_ref[...], w_in_ref[D : 2 * D]).astype(BF)
        halo = halo_out[...]
    edges = edge_ref[first : first + HALF]
    recv_hot = one_hot(column_of(recv_ref, first, HALF), NODES)
    send_hot = one_hot(column_of(send_ref, first, HALF), NODES + 2 * BORDER)
    pre = dot(edges, w_in_ref[:D])
    pre = pre + dot(jnp.concatenate([recv_hot, send_hot[:, :NODES]], axis=1), table_ref[...])
    pre = pre + dot(send_hot[:, NODES:], halo)
    rows_ref[...] = finish_edges(pre, edges, w_out_ref[...], gain_ref[...])
    copy = pltpu.make_async_copy(rows_ref, new_ref.at[pl.ds(first, HALF)], sem)
    copy.start()
    sums = dot(one_hot_rows(recv_ref, first, HALF, NODES), rows_ref[...])
    sum_ref[...] = before_ref[...] + sums if first else sums
    copy.wait()


def gather_kernel(send_ref, recv_ref, table_ref, send_out, recv_out):
    for first in range(0, EDGES, BLOCK):
        rows = slice(first, first + BLOCK)
        for ids_ref, out_ref in ((send_ref, send_out), (recv_ref, recv_out)):
            hot = one_hot(column_of(ids_ref, first, BLOCK), table_ref.shape[0])
            out_ref[rows] = dot(hot, table_ref[...]).astype(BF)


def coarse_kernel(
    edge_ref, send_ref, recv_ref, slot_ref, table_ref, send_part, recv_part, w_in_ref, w_out_ref,
    gain_ref, new_ref, sum_ref, rows_ref, sems,
):
    gain = gain_ref[...]
    half = table_ref.shape[0]
    copies = []
    for at in range(EDGES // BLOCK):
        rows = slice(at * BLOCK, (at + 1) * BLOCK)
        edges = edge_ref[rows]
        joined = [edges]
        for ids_ref, part_ref in ((send_ref, send_part), (recv_ref, recv_part)):
            hot = one_hot(column_of(ids_ref, at * BLOCK, BLOCK), half, half)
            joined.append((dot(hot, table_ref[...]) + part_ref[rows].astype(F32)).astype(BF))
        pre = dot(jnp.concatenate(joined, axis=1), w_in_ref[...])
        rows_ref[rows] = finish_edges(pre, edges, w_out_ref[...], gain)
        copies.append(send_rows(rows_ref, new_ref, sems, at))
    hot = one_hot_rows(slot_ref, 0, EDGES, sum_ref.shape[0])
    sum_ref[...] = dot(hot, rows_ref[...]).astype(BF)
    for copy in copies:
        copy.wait()


def finish_nodes(pre, nodes, w_out_ref, gain):
    projected = dot(silu(pre).astype(BF), w_out_ref[...])
    return (nodes.astype(F32) + layer_norm(projected) * gain).astype(BF)


def node_kernel(node_ref, sum_ref, w_in_ref, w_out_ref, gain_ref, out_ref, first_ref, pre_ref):
    nodes = node_ref[...]
    pre = dot(nodes, w_in_ref[:D])
    pre_ref[...] = pre[:TAIL]
    first_ref[...] = sum_ref[:TAIL]
    pre = pre + dot(sum_ref[...].astype(BF), w_in_ref[D:])
    out_ref[...] = finish_nodes(pre, nodes, w_out_ref, gain_ref[...])


def tail_kernel(
    node_ref, sum_ref, pre_ref, parts_ref, w_in_ref, w_out_ref, gain_ref, _, out_ref, rows_ref, sem
):
    parts = parts_ref[...].astype(F32).reshape(-1, COARSE_ROWS, D)
    total = sum_ref[...]
    total = jnp.concatenate(
        [total[:COARSE_ROWS] + jnp.sum(parts, axis=0), total[COARSE_ROWS:]], axis=0
    )
    pre = pre_ref[...] + dot(total.astype(BF), w_in_ref[D:])
    rows_ref[...] = finish_nodes(pre, node_ref[:TAIL], w_out_ref, gain_ref[...])
    copy = pltpu.make_async_copy(rows_ref, out_ref.at[pl.ds(0, TAIL)], sem)
    copy.start()
    copy.wait()


def shape(rows, dtype=BF):
    return jax.ShapeDtypeStruct((rows, D), dtype)


VMEM_SPEC = pl.BlockSpec(memory_space=pltpu.VMEM)
ANY_SPEC = pl.BlockSpec(memory_space=pl.ANY)
HBM_SPEC = pl.BlockSpec(memory_space=pltpu.HBM)


def call(
    kernel, outs, flops, *args, name, scratch=(), out_any=(), in_any=(), aliases=None, spec=ANY_SPEC
):
    return pl.pallas_call(
        kernel,
        out_shape=outs,
        in_specs=[spec if at in in_any else VMEM_SPEC for at in range(len(args))],
        out_specs=tuple(
            ANY_SPEC if at in out_any else VMEM_SPEC for at in range(len(outs))
        ),
        scratch_shapes=scratch,
        input_output_aliases=aliases or {},
        compiler_params=pltpu.CompilerParams(vmem_limit_bytes=VMEM_LIMIT),
        cost_estimate=pl.CostEstimate(flops=flops, bytes_accessed=4 << 20, transcendentals=0),
        name=name,
    )(*args)


def patch_pairs(move):
    pairs = []
    for x in range(SIDE):
        for y in range(SIDE):
            for core in range(CORES):
                to_x, to_y, to_core = move(x, y, core)
                pairs.append(
                    ((x * SIDE + y) * CORES + core, (to_x * SIDE + to_y) * CORES + to_core)
                )
    return pairs


def crossed(k, turn):
    return patch_pairs(lambda x, y, c: (x ^ k, y, c) if c == turn else (x, y ^ k, c))


SWAP_CORE = patch_pairs(lambda x, y, c: (x, y, c ^ 1))


def along_z(move):
    pairs = []
    for group in range(GROUPS):
        pair, member = move(group >> 1, group & 1)
        target = ((pair % (GROUPS // 2)) << 1 | member) * PATCHES
        pairs += [(group * PATCHES + i, target + (i ^ 1)) for i in range(PATCHES)]
    return pairs


Z_PAIR = along_z(lambda pair, member: (pair, member ^ 1))
Z_FAR = along_z(lambda pair, member: (pair + 2, member ^ 1))
Z_MID = along_z(lambda pair, member: (pair - 1 + 2 * member, member))
Z_NEAR = along_z(lambda pair, member: (pair - 1 + 2 * member, member ^ 1))
OUTER = [(i, (i + 1 if i & 1 else i - 1) % PATCHES) for i in range(PATCHES)]
tie = lambda *arrays: lax.optimization_barrier(arrays)


def place_z(group, mine):
    away = ((group >> 1) - (mine >> 1)) * jnp.where(mine & 1 == 0, 1, -1) & 3
    high = away >> 1
    place = ((away ^ high) & 1) << 2 | high << 1 | ((group ^ mine) & 1 ^ high)
    return place, (place & 1) ^ jnp.where(place >= 2, 1, 0)


def shards(
    node_lat, fine_edge_lat, fine_send, fine_recv, border_rows, coarse_edge_lat, coarse_send,
    coarse_recv, w_edge_in, w_edge_out, edge_gain, w_node_in, w_node_out, node_gain,
):
    group = lax.axis_index("group")
    patch = lax.axis_index("patch")
    my_core, my_y, my_x = patch & 1, patch >> 1 & 3, patch >> 3
    edge_gain = edge_gain[None, :]
    node_gain = node_gain[None, :]
    grid = lambda ids: ids.reshape(-1, 128)
    swap = lambda rows, pairs: lax.ppermute(rows, "patch", pairs)
    join = lambda *rows: jnp.concatenate(rows, axis=0)

    turn = lambda away: away ^ (away >> 1)

    def place(ids):
        row, at = ids & 7, ids >> 3
        core, y, x = at & 1, turn(at >> 1 & 3 ^ my_y), turn(at >> 3 & 3 ^ my_x)
        z, exchanged = place_z(at >> 5, group)
        half = core ^ my_core ^ exchanged
        x_first = half == my_core
        first, second = jnp.where(x_first, x, y), jnp.where(x_first, y, x)
        return half << 10 | second << 8 | first << 6 | z << 3 | row

    send_place, recv_place = grid(place(coarse_send)), grid(place(coarse_recv))
    slot = grid(jnp.where(coarse_recv >> 8 == group, coarse_recv & 255, -1))
    fine_place = grid(
        jnp.where((fine_send >= NODES) & (my_core == 0), fine_send ^ BORDER, fine_send)
    )
    in_hbm = lambda *arrays: [pltpu.with_memory_space_constraint(a, pltpu.HBM) for a in arrays]
    like = lambda *arrays: [jax.ShapeDtypeStruct(a.shape, a.dtype) for a in arrays]

    own = node_lat[:COARSE_ROWS]
    own, *loads = tie(own, border_rows, node_lat, w_edge_in, w_edge_out)
    loads[0] = grid(loads[0])
    pair = lax.ppermute(own, ("group", "patch"), Z_PAIR)
    inner, outer, nodes, w_in, w_out = call(
        pick_kernel, [shape(BORDER), shape(BORDER), *like(*loads[1:])], 2 * 256 * 512 * 512,
        *in_hbm(*loads), name="pick",
        scratch=[pltpu.VMEM((2, BORDER), jnp.int32), pltpu.SemaphoreType.DMA((4,))],
        in_any=range(4), spec=HBM_SPEC,
    )
    pair, inner, outer, nodes, w_in, w_out = tie(pair, inner, outer, nodes, w_in, w_out)
    near = join(own, pair)
    near, inner, outer, nodes = tie(near, inner, outer, nodes)
    others = [lax.ppermute(near, ("group", "patch"), to) for to in (Z_NEAR, Z_MID, Z_FAR)]
    inner, outer = swap(inner, SWAP_CORE), swap(outer, OUTER)
    (table,) = call(
        project_kernel, (shape(2 * NODES),), 4 * 512 * 512 * 512, nodes, w_in, name="project"
    )
    *others, table = tie(*others, table)
    block = join(near, *others)

    block, table = tie(block, table)
    others = [swap(block, crossed(k, 0)) for k in (1, 3, 2)]
    fine_args = (
        fine_edge_lat, fine_place, grid(fine_recv), table, inner, outer, w_in, w_out, edge_gain
    )
    fine_scratch = [pltpu.VMEM((HALF, D), BF), pltpu.SemaphoreType.DMA]
    fine_new, fine_sum, halo = call(
        functools.partial(fine_kernel, 0), (shape(EDGES), shape(NODES, F32), shape(2 * BORDER)),
        2 << 30, *fine_args, name="fine_first", scratch=fine_scratch, out_any=(0,),
    )
    *others, fine_sum = tie(*others, fine_sum)
    block = join(block, *others)

    block, fine_sum = tie(block, fine_sum)
    others = [swap(block, crossed(k, 1)) for k in (1, 3, 2)]
    fine_new, fine_sum = call(
        functools.partial(fine_kernel, HALF), (shape(EDGES), shape(NODES, F32)), 2 << 30,
        *fine_args, halo, fine_sum, fine_new, name="fine_second", scratch=fine_scratch,
        out_any=(0,), in_any=(len(fine_args) + 2,), aliases={len(fine_args) + 2: 0},
    )
    node_main, first_sum, first_pre = call(
        node_kernel, (shape(NODES), shape(TAIL, F32), shape(TAIL, F32)), 768 << 20, nodes,
        fine_sum, w_node_in, w_node_out, node_gain, name="node",
    )
    *others, first_sum = tie(*others, first_sum)
    part = join(block, *others)
    other_half = swap(part, SWAP_CORE)

    send_part, recv_part = call(
        gather_kernel, (shape(EDGES), shape(EDGES)), 2 << 30, send_place, recv_place, part,
        name="gather",
    )
    coarse_new, sums = call(
        coarse_kernel, (shape(EDGES), shape(PATCHES * COARSE_ROWS)), 4 << 30, coarse_edge_lat,
        send_place, recv_place, slot, other_half, send_part, recv_part, w_in, w_out, edge_gain,
        name="coarse",
        scratch=[pltpu.VMEM((EDGES, D), BF), pltpu.SemaphoreType.DMA((EDGES // BLOCK,))],
        out_any=(0,),
    )

    parts = lax.all_to_all(sums.reshape(PATCHES, COARSE_ROWS, D), "patch", 0, 0)
    (node_new,) = call(
        tail_kernel, (shape(NODES),), 24 << 20, nodes, first_sum, first_pre, parts.reshape(-1, D),
        w_node_in, w_node_out, node_gain, node_main, name="tail",
        scratch=[pltpu.VMEM((TAIL, D), BF), pltpu.SemaphoreType.DMA], out_any=(0,), in_any=(7,),
        aliases={7: 0},
    )
    return (node_new, fine_new, coarse_new)


def solution(mesh):
    in_specs = (
        P(("group", "patch"), None), P(("group", "patch"), None), P(("group", "patch")),
        P(("group", "patch")), P(("group", "patch")), P("patch", None), P("patch"), P("patch"),
        P(), P(), P(), P(), P(), P(),
    )
    out_specs = (P(("group", "patch"), None), P(("group", "patch"), None), P("patch", None))
    return jax.shard_map(shards, mesh=mesh, in_specs=in_specs, out_specs=out_specs, check_vma=False)
```

```python
import functools

import jax
import jax.numpy as jnp
from jax import lax
from jax.experimental import pallas as pl
from jax.experimental.pallas import tpu as pltpu
from jax.sharding import PartitionSpec as P

D = 512
GROUPS = 8
SIDE = 4
CORES = 2
PATCHES = SIDE * SIDE * CORES
BORDER = 128
COARSE_ROWS = 8
EDGES = 1024
HALF = 512
NODES = 512
TAIL = 16
EPS = 1e-05
BF = jnp.bfloat16
F32 = jnp.float32
VMEM_LIMIT = 10 * 1024 * 1024


def dot(a, b):
    return jnp.dot(a, b, preferred_element_type=F32)


def silu(values):
    half = 0.5 * values
    return half * jnp.tanh(half) + half


def layer_norm(values):
    average = jnp.mean(values, axis=-1, keepdims=True)
    centred = values - average
    variance = jnp.mean(centred * centred, axis=-1, keepdims=True)
    return centred * lax.rsqrt(variance + EPS)


def column_of(ids_ref, first, rows):
    tiles = []
    for at in range(first // 128, (first + rows) // 128):
        row = jnp.broadcast_to(ids_ref[at : at + 1, :], (128, 128))
        tiles.append(row.T)
    return jnp.concatenate(tiles, axis=0).astype(jnp.int16)


def one_hot(column, width, offset=0):
    lanes = lax.broadcasted_iota(jnp.int16, column.shape, 1)
    one, zero = jnp.ones(column.shape, BF), jnp.zeros(column.shape, BF)
    return jnp.concatenate(
        [
            jnp.where(column == lanes + jnp.int16(offset + 128 * at), one, zero)
            for at in range(width // 128)
        ],
        axis=1,
    )


def one_hot_rows(ids_ref, first, count, height):
    rows = lax.broadcasted_iota(jnp.int16, (height, 128), 0)
    one, zero = jnp.ones((height, 128), BF), jnp.zeros((height, 128), BF)
    parts = []
    for at in range(first // 128, (first + count) // 128):
        ids = jnp.broadcast_to(ids_ref[at : at + 1, :], (height, 128)).astype(jnp.int16)
        parts.append(jnp.where(ids == rows, one, zero))
    return jnp.concatenate(parts, axis=1)


def finish_edges(pre, edges, w_out, gain):
    hidden = silu(pre).astype(BF)
    projected = dot(hidden, w_out)
    return (edges.astype(F32) + layer_norm(projected) * gain).astype(BF)


def pick_kernel(
    border_in, node_in, w_in, inner_ref, outer_ref, node_ref, w_in_ref, border_ref, sems
):
    copies = [
        pltpu.make_async_copy(source, target, sems.at[at])
        for at, (source, target) in enumerate(
            (
                (border_in, border_ref), (node_in, node_ref), (w_in, w_in_ref)
            )
        )
    ]
    for copy in copies:
        copy.start()
    copies[0].wait()
    hot = one_hot(column_of(border_ref, 0, 2 * BORDER), NODES)
    copies[1].wait()
    picked = dot(hot, node_ref[...]).astype(BF)
    lower, upper = picked[:BORDER], picked[BORDER:]
    on_first = lax.axis_index("patch") % CORES == 0
    inner_ref[...] = jnp.where(on_first, upper, lower)
    outer_ref[...] = jnp.where(on_first, lower, upper)
    for copy in copies[2:]:
        copy.wait()


def project_kernel(node_ref, w_ref, out_ref):
    nodes = node_ref[...]
    out_ref[:NODES] = dot(nodes, w_ref[2 * D :]).astype(BF)
    out_ref[NODES:] = dot(nodes, w_ref[D : 2 * D]).astype(BF)


def fine_kernel(
    first, edge_ref, send_ref, recv_ref, table_ref, inner_ref, outer_ref, w_in_ref, w_out_ref,
    gain_ref, *rest,
):
    if first:
        halo_in, before_ref, _, new_ref, sum_ref, rows_ref, sem = rest
        halo = halo_in[...]
    else:
        new_ref, sum_ref, halo_out, rows_ref, sem = rest
        halo_out[:BORDER] = dot(inner_ref[...], w_in_ref[D : 2 * D]).astype(BF)
        halo_out[BORDER:] = dot(outer_ref[...], w_in_ref[D : 2 * D]).astype(BF)
        halo = halo_out[...]
    edges = edge_ref[first : first + HALF]
    senders = send_ref[...]
    on_first = lax.axis_index("patch") % CORES == 0
    senders = jnp.where((senders >= NODES) & on_first, senders ^ BORDER, senders)
    recv_hot = one_hot(column_of(recv_ref, first, HALF), NODES)
    send_hot = one_hot(column_of(senders, first, HALF), NODES + 2 * BORDER)
    pre = dot(edges, w_in_ref[:D])
    pre = pre + dot(jnp.concatenate([recv_hot, send_hot[:, :NODES]], axis=1), table_ref[...])
    pre = pre + dot(send_hot[:, NODES:], halo)
    rows_ref[...] = finish_edges(pre, edges, w_out_ref[...], gain_ref[...])
    copy = pltpu.make_async_copy(rows_ref, new_ref.at[pl.ds(first, HALF)], sem)
    copy.start()
    sums = dot(one_hot_rows(recv_ref, first, HALF, NODES), rows_ref[...])
    sum_ref[...] = before_ref[...] + sums if first else sums
    copy.wait()


def place_z(group, mine):
    away = ((group >> 1) - (mine >> 1)) * jnp.where(mine & 1 == 0, 1, -1) & 3
    high = away >> 1
    place = ((away ^ high) & 1) << 2 | high << 1 | ((group ^ mine) & 1 ^ high)
    return place, (place & 1) ^ jnp.where(place >= 2, 1, 0)


def place(ids):
    group, patch = lax.axis_index("group"), lax.axis_index("patch")
    my_core, my_y, my_x = patch & 1, patch >> 1 & 3, patch >> 3
    row, at = ids & 7, ids >> 3
    turn = lambda away: away ^ (away >> 1)
    core, y, x = at & 1, turn(at >> 1 & 3 ^ my_y), turn(at >> 3 & 3 ^ my_x)
    z, exchanged = place_z(at >> 5, group)
    half = core ^ my_core ^ exchanged
    x_first = half == my_core
    first, second = jnp.where(x_first, x, y), jnp.where(x_first, y, x)
    return half << 10 | second << 8 | first << 6 | z << 3 | row


def gather_kernel(
    send_ref, recv_ref, table_ref, send_place, recv_place, send_out, recv_out
):
    for ids_ref, place_ref, out_ref in (
        (send_ref, send_place, send_out), (recv_ref, recv_place, recv_out)
    ):
        place_ref[...] = place(ids_ref[...])
        hot = one_hot(column_of(place_ref, 0, EDGES), table_ref.shape[0])
        out_ref[...] = dot(hot, table_ref[...]).astype(BF)


def coarse_kernel(
    edge_ref, send_ref, recv_ref, node_ref, table_ref, send_part, recv_part, w_in_ref, w_out_ref,
    gain_ref, new_ref, sum_ref, rows_ref, slot_ref, sem,
):
    half = table_ref.shape[0]
    edges = edge_ref[...]
    joined = [edges]
    for ids_ref, part_ref in ((send_ref, send_part), (recv_ref, recv_part)):
        hot = one_hot(column_of(ids_ref, 0, EDGES), half, half)
        joined.append((dot(hot, table_ref[...]) + part_ref[...].astype(F32)).astype(BF))
    pre = dot(jnp.concatenate(joined, axis=1), w_in_ref[...])
    rows_ref[...] = finish_edges(pre, edges, w_out_ref[...], gain_ref[...])
    copy = pltpu.make_async_copy(rows_ref, new_ref, sem)
    copy.start()
    nodes = node_ref[...]
    slot_ref[...] = jnp.where(nodes >> 8 == lax.axis_index("group"), nodes & 255, -1)
    hot = one_hot_rows(slot_ref, 0, EDGES, sum_ref.shape[0])
    sum_ref[...] = dot(hot, rows_ref[...]).astype(BF)
    copy.wait()


def finish_nodes(pre, nodes, w_out_ref, gain):
    projected = dot(silu(pre).astype(BF), w_out_ref[...])
    return (nodes.astype(F32) + layer_norm(projected) * gain).astype(BF)


def node_kernel(node_ref, sum_ref, w_in_ref, w_out_ref, gain_ref, out_ref, first_ref, pre_ref):
    nodes = node_ref[...]
    pre = dot(nodes, w_in_ref[:D])
    pre_ref[...] = pre[:TAIL]
    first_ref[...] = sum_ref[:TAIL]
    pre = pre + dot(sum_ref[...].astype(BF), w_in_ref[D:])
    out_ref[...] = finish_nodes(pre, nodes, w_out_ref, gain_ref[...])


def tail_kernel(
    node_ref, sum_ref, pre_ref, parts_ref, w_in_ref, w_out_ref, gain_ref, _, out_ref, rows_ref, sem
):
    parts = parts_ref[...].astype(F32).reshape(-1, COARSE_ROWS, D)
    total = sum_ref[...]
    total = jnp.concatenate(
        [total[:COARSE_ROWS] + jnp.sum(parts, axis=0), total[COARSE_ROWS:]], axis=0
    )
    pre = pre_ref[...] + dot(total.astype(BF), w_in_ref[D:])
    rows_ref[...] = finish_nodes(pre, node_ref[:TAIL], w_out_ref, gain_ref[...])
    copy = pltpu.make_async_copy(rows_ref, out_ref.at[pl.ds(0, TAIL)], sem)
    copy.start()
    copy.wait()


def shape(rows, dtype=BF):
    return jax.ShapeDtypeStruct((rows, D), dtype)


VMEM_SPEC = pl.BlockSpec(memory_space=pltpu.VMEM)
ANY_SPEC = pl.BlockSpec(memory_space=pl.ANY)
HBM_SPEC = pl.BlockSpec(memory_space=pltpu.HBM)


def call(
    kernel, outs, flops, *args, name, scratch=(), out_any=(), in_any=(), aliases=None, spec=ANY_SPEC
):
    return pl.pallas_call(
        kernel,
        out_shape=outs,
        in_specs=[spec if at in in_any else VMEM_SPEC for at in range(len(args))],
        out_specs=tuple(
            ANY_SPEC if at in out_any else VMEM_SPEC for at in range(len(outs))
        ),
        scratch_shapes=scratch,
        input_output_aliases=aliases or {},
        compiler_params=pltpu.CompilerParams(vmem_limit_bytes=VMEM_LIMIT),
        cost_estimate=pl.CostEstimate(flops=flops, bytes_accessed=4 << 20, transcendentals=0),
        name=name,
    )(*args)


def patch_pairs(move):
    pairs = []
    for x in range(SIDE):
        for y in range(SIDE):
            for core in range(CORES):
                to_x, to_y, to_core = move(x, y, core)
                pairs.append(
                    ((x * SIDE + y) * CORES + core, (to_x * SIDE + to_y) * CORES + to_core)
                )
    return pairs


def crossed(k, turn):
    return patch_pairs(lambda x, y, c: (x ^ k, y, c) if c == turn else (x, y ^ k, c))


SWAP_CORE = patch_pairs(lambda x, y, c: (x, y, c ^ 1))


def along_z(move):
    pairs = []
    for group in range(GROUPS):
        pair, member = move(group >> 1, group & 1)
        target = ((pair % (GROUPS // 2)) << 1 | member) * PATCHES
        pairs += [(group * PATCHES + i, target + (i ^ 1)) for i in range(PATCHES)]
    return pairs


Z_PAIR = along_z(lambda pair, member: (pair, member ^ 1))
Z_FAR = along_z(lambda pair, member: (pair + 2, member ^ 1))
Z_MID = along_z(lambda pair, member: (pair - 1 + 2 * member, member))
Z_NEAR = along_z(lambda pair, member: (pair - 1 + 2 * member, member ^ 1))
OUTER = [(i, (i + 1 if i & 1 else i - 1) % PATCHES) for i in range(PATCHES)]
tie = lambda *arrays: lax.optimization_barrier(arrays)


def shards(
    node_lat, fine_edge_lat, fine_send, fine_recv, border_rows, coarse_edge_lat, coarse_send,
    coarse_recv, w_edge_in, w_edge_out, edge_gain, w_node_in, w_node_out, node_gain,
):
    edge_gain = edge_gain[None, :]
    node_gain = node_gain[None, :]
    grid = lambda ids: ids.reshape(-1, 128)
    swap = lambda rows, pairs: lax.ppermute(rows, "patch", pairs)
    join = lambda *rows: jnp.concatenate(rows, axis=0)

    in_hbm = lambda *arrays: [pltpu.with_memory_space_constraint(a, pltpu.HBM) for a in arrays]
    like = lambda *arrays: [jax.ShapeDtypeStruct(a.shape, a.dtype) for a in arrays]

    own = node_lat[:COARSE_ROWS]
    own, *loads = tie(own, border_rows, node_lat, w_edge_in)
    loads[0] = grid(loads[0])
    pair = lax.ppermute(own, ("group", "patch"), Z_PAIR)
    inner, outer, nodes, w_in = call(
        pick_kernel, [shape(BORDER), shape(BORDER), *like(*loads[1:])], 2 * 256 * 512 * 512,
        *in_hbm(*loads), name="pick",
        scratch=[pltpu.VMEM((2, BORDER), jnp.int32), pltpu.SemaphoreType.DMA((3,))],
        in_any=range(3), spec=HBM_SPEC,
    )
    pair, inner, outer, nodes, w_in = tie(pair, inner, outer, nodes, w_in)
    near = join(own, pair)
    near, inner, outer, nodes = tie(near, inner, outer, nodes)
    others = [lax.ppermute(near, ("group", "patch"), to) for to in (Z_NEAR, Z_MID, Z_FAR)]
    inner, outer = swap(inner, SWAP_CORE), swap(outer, OUTER)
    (table,) = call(
        project_kernel, (shape(2 * NODES),), 4 * 512 * 512 * 512, nodes, w_in, name="project"
    )
    *others, table = tie(*others, table)
    block = join(near, *others)

    block, table = tie(block, table)
    others = [swap(block, crossed(k, 0)) for k in (1, 3, 2)]
    fine_args = (
        fine_edge_lat, grid(fine_send), grid(fine_recv), table, inner, outer, w_in, w_edge_out, edge_gain
    )
    fine_scratch = [pltpu.VMEM((HALF, D), BF), pltpu.SemaphoreType.DMA]
    fine_new, fine_sum, halo = call(
        functools.partial(fine_kernel, 0), (shape(EDGES), shape(NODES, F32), shape(2 * BORDER)),
        2 << 30, *fine_args, name="fine_first", scratch=fine_scratch, out_any=(0,),
    )
    *others, fine_sum = tie(*others, fine_sum)
    block = join(block, *others)

    block, fine_sum = tie(block, fine_sum)
    others = [swap(block, crossed(k, 1)) for k in (1, 3, 2)]
    fine_new, fine_sum = call(
        functools.partial(fine_kernel, HALF), (shape(EDGES), shape(NODES, F32)), 2 << 30,
        *fine_args, halo, fine_sum, fine_new, name="fine_second", scratch=fine_scratch,
        out_any=(0,), in_any=(len(fine_args) + 2,), aliases={len(fine_args) + 2: 0},
    )
    node_main, first_sum, first_pre = call(
        node_kernel, (shape(NODES), shape(TAIL, F32), shape(TAIL, F32)), 768 << 20, nodes,
        fine_sum, w_node_in, w_node_out, node_gain, name="node",
    )
    *others, first_sum = tie(*others, first_sum)
    part = join(block, *others)
    other_half = swap(part, SWAP_CORE)

    ids = jax.ShapeDtypeStruct((EDGES // 128, 128), jnp.int32)
    send_place, recv_place, send_part, recv_part = call(
        gather_kernel, (ids, ids, shape(EDGES), shape(EDGES)), 2 << 30, grid(coarse_send),
        grid(coarse_recv), part, name="gather",
    )
    coarse_new, sums = call(
        coarse_kernel, (shape(EDGES), shape(PATCHES * COARSE_ROWS)), 4 << 30, coarse_edge_lat,
        send_place, recv_place, grid(coarse_recv), other_half, send_part, recv_part, w_in,
        w_edge_out, edge_gain, name="coarse",
        scratch=[
            pltpu.VMEM((EDGES, D), BF), pltpu.VMEM((EDGES // 128, 128), jnp.int32),
            pltpu.SemaphoreType.DMA,
        ],
        out_any=(0,),
    )

    parts = lax.all_to_all(sums.reshape(PATCHES, COARSE_ROWS, D), "patch", 0, 0)
    (node_new,) = call(
        tail_kernel, (shape(NODES),), 24 << 20, nodes, first_sum, first_pre, parts.reshape(-1, D),
        w_node_in, w_node_out, node_gain, node_main, name="tail",
        scratch=[pltpu.VMEM((TAIL, D), BF), pltpu.SemaphoreType.DMA], out_any=(0,), in_any=(7,),
        aliases={7: 0},
    )
    return (node_new, fine_new, coarse_new)


def solution(mesh):
    in_specs = (
        P(("group", "patch"), None), P(("group", "patch"), None), P(("group", "patch")),
        P(("group", "patch")), P(("group", "patch")), P("patch", None), P("patch"), P("patch"),
        P(), P(), P(), P(), P(), P(),
    )
    out_specs = (P(("group", "patch"), None), P(("group", "patch"), None), P("patch", None))
    return jax.shard_map(shards, mesh=mesh, in_specs=in_specs, out_specs=out_specs, check_vma=False)
```

```python
import functools

import jax
import jax.numpy as jnp
from jax import lax
from jax.experimental import pallas as pl
from jax.experimental.pallas import tpu as pltpu
from jax.sharding import PartitionSpec as P

D = 512
GROUPS = 8
SIDE = 4
CORES = 2
PATCHES = SIDE * SIDE * CORES
BORDER = 128
COARSE_ROWS = 8
EDGES = 1024
HALF = 512
EARLY = 256
NODES = 512
TAIL = 16
EPS = 1e-05
BF = jnp.bfloat16
F32 = jnp.float32
VMEM_LIMIT = 10 * 1024 * 1024


def dot(a, b):
    return jnp.dot(a, b, preferred_element_type=F32)


def silu(values):
    half = 0.5 * values
    return half * jnp.tanh(half) + half


def layer_norm(values):
    average = jnp.mean(values, axis=-1, keepdims=True)
    centred = values - average
    variance = jnp.mean(centred * centred, axis=-1, keepdims=True)
    return centred * lax.rsqrt(variance + EPS)


def column_of(ids_ref, first, rows):
    tiles = []
    for at in range(first // 128, (first + rows) // 128):
        row = jnp.broadcast_to(ids_ref[at : at + 1, :], (128, 128))
        tiles.append(row.T)
    return jnp.concatenate(tiles, axis=0).astype(jnp.int16)


def one_hot(column, width, offset=0):
    lanes = lax.broadcasted_iota(jnp.int16, column.shape, 1)
    one, zero = jnp.ones(column.shape, BF), jnp.zeros(column.shape, BF)
    return jnp.concatenate(
        [
            jnp.where(column == lanes + jnp.int16(offset + 128 * at), one, zero)
            for at in range(width // 128)
        ],
        axis=1,
    )


def one_hot_rows(ids_ref, first, count, height):
    rows = lax.broadcasted_iota(jnp.int16, (height, 128), 0)
    one, zero = jnp.ones((height, 128), BF), jnp.zeros((height, 128), BF)
    parts = []
    for at in range(first // 128, (first + count) // 128):
        ids = jnp.broadcast_to(ids_ref[at : at + 1, :], (height, 128)).astype(jnp.int16)
        parts.append(jnp.where(ids == rows, one, zero))
    return jnp.concatenate(parts, axis=1)


def put_rows(rows_ref, out_ref, first, sem):
    copy = pltpu.make_async_copy(rows_ref, out_ref.at[pl.ds(first, rows_ref.shape[0])], sem)
    copy.start()
    return copy


def finish_edges(pre, edges, w_out, gain):
    hidden = silu(pre).astype(BF)
    projected = dot(hidden, w_out)
    return (edges.astype(F32) + layer_norm(projected) * gain).astype(BF)


def pick_kernel(
    border_in, node_in, w_in, inner_ref, outer_ref, node_ref, w_in_ref, border_ref, sems
):
    copies = [
        pltpu.make_async_copy(source, target, sems.at[at])
        for at, (source, target) in enumerate(
            (
                (border_in, border_ref), (node_in, node_ref), (w_in, w_in_ref)
            )
        )
    ]
    for copy in copies:
        copy.start()
    copies[0].wait()
    hot = one_hot(column_of(border_ref, 0, 2 * BORDER), NODES)
    copies[1].wait()
    picked = dot(hot, node_ref[...]).astype(BF)
    lower, upper = picked[:BORDER], picked[BORDER:]
    on_first = lax.axis_index("patch") % CORES == 0
    inner_ref[...] = jnp.where(on_first, upper, lower)
    outer_ref[...] = jnp.where(on_first, lower, upper)
    for copy in copies[2:]:
        copy.wait()


def project_kernel(node_ref, w_ref, out_ref):
    nodes = node_ref[...]
    out_ref[:NODES] = dot(nodes, w_ref[2 * D :]).astype(BF)
    out_ref[NODES:] = dot(nodes, w_ref[D : 2 * D]).astype(BF)


def fine_kernel(
    first, edge_ref, send_ref, recv_ref, table_ref, inner_ref, outer_ref, w_in_ref, w_out_ref,
    gain_ref, *rest,
):
    if first:
        halo_in, before_ref, earlier_ref, rows_ref, sum_ref, new_ref, sem = rest
        copy = put_rows(earlier_ref, new_ref, 0, sem)
        halo = halo_in[...]
    else:
        rows_ref, sum_ref, halo_out = rest
        halo_out[:BORDER] = dot(inner_ref[...], w_in_ref[D : 2 * D]).astype(BF)
        halo_out[BORDER:] = dot(outer_ref[...], w_in_ref[D : 2 * D]).astype(BF)
        halo = halo_out[...]
    edges = edge_ref[first : first + HALF]
    senders = send_ref[...]
    on_first = lax.axis_index("patch") % CORES == 0
    senders = jnp.where((senders >= NODES) & on_first, senders ^ BORDER, senders)
    recv_hot = one_hot(column_of(recv_ref, first, HALF), NODES)
    send_hot = one_hot(column_of(senders, first, HALF), NODES + 2 * BORDER)
    pre = dot(edges, w_in_ref[:D])
    pre = pre + dot(jnp.concatenate([recv_hot, send_hot[:, :NODES]], axis=1), table_ref[...])
    pre = pre + dot(send_hot[:, NODES:], halo)
    rows_ref[...] = finish_edges(pre, edges, w_out_ref[...], gain_ref[...])
    sums = dot(one_hot_rows(recv_ref, first, HALF, NODES), rows_ref[...])
    sum_ref[...] = before_ref[...] + sums if first else sums
    if first:
        copy.wait()


def place_z(group, mine):
    away = ((group >> 1) - (mine >> 1)) * jnp.where(mine & 1 == 0, 1, -1) & 3
    high = away >> 1
    place = ((away ^ high) & 1) << 2 | high << 1 | ((group ^ mine) & 1 ^ high)
    return place, (place & 1) ^ jnp.where(place >= 2, 1, 0)


def place(ids):
    group, patch = lax.axis_index("group"), lax.axis_index("patch")
    my_core, my_y, my_x = patch & 1, patch >> 1 & 3, patch >> 3
    row, at = ids & 7, ids >> 3
    turn = lambda away: away ^ (away >> 1)
    core, y, x = at & 1, turn(at >> 1 & 3 ^ my_y), turn(at >> 3 & 3 ^ my_x)
    z, exchanged = place_z(at >> 5, group)
    half = core ^ my_core ^ exchanged
    x_first = half == my_core
    first, second = jnp.where(x_first, x, y), jnp.where(x_first, y, x)
    return half << 10 | second << 8 | first << 6 | z << 3 | row


def early_kernel(
    edge_ref, send_ref, recv_ref, mine_ref, theirs_ref, w_in_ref, send_place, recv_place,
    send_out, recv_out, pre_ref, table_ref,
):
    table_ref[:EARLY] = mine_ref[...]
    table_ref[EARLY:] = theirs_ref[...]
    pre_ref[...] = dot(edge_ref[...], w_in_ref[:D])
    for ids_ref, place_ref, out_ref in (
        (send_ref, send_place, send_out), (recv_ref, recv_place, recv_out)
    ):
        place_ref[...] = place(ids_ref[...])
        column = column_of(place_ref, 0, EDGES)
        hot = [one_hot(column, EARLY, first) for first in (0, SIDE * EARLY)]
        out_ref[...] = dot(jnp.concatenate(hot, axis=1), table_ref[...]).astype(BF)


def gather_kernel(
    send_ref, recv_ref, send_part, recv_part, table_ref, rows_ref, send_out, recv_out, new_ref, sem
):
    copy = put_rows(rows_ref, new_ref, 0, sem)
    for ids_ref, part_ref, out_ref in (
        (send_ref, send_part, send_out), (recv_ref, recv_part, recv_out)
    ):
        hot = one_hot(column_of(ids_ref, 0, EDGES), table_ref.shape[0], EARLY)
        out_ref[...] = (dot(hot, table_ref[...]) + part_ref[...].astype(F32)).astype(BF)
    copy.wait()


def coarse_kernel(
    edge_ref, pre_ref, send_ref, recv_ref, node_ref, table_ref, send_part, recv_part, w_in_ref,
    w_out_ref, gain_ref, rows_ref, sum_ref, slot_ref,
):
    joined = []
    for ids_ref, part_ref in ((send_ref, send_part), (recv_ref, recv_part)):
        hot = one_hot(column_of(ids_ref, 0, EDGES), table_ref.shape[0], (SIDE + 1) * EARLY)
        joined.append((dot(hot, table_ref[...]) + part_ref[...].astype(F32)).astype(BF))
    pre = pre_ref[...] + dot(jnp.concatenate(joined, axis=1), w_in_ref[D:])
    rows_ref[...] = finish_edges(pre, edge_ref[...], w_out_ref[...], gain_ref[...])
    nodes = node_ref[...]
    slot_ref[...] = jnp.where(nodes >> 8 == lax.axis_index("group"), nodes & 255, -1)
    hot = one_hot_rows(slot_ref, 0, EDGES, sum_ref.shape[0])
    sum_ref[...] = dot(hot, rows_ref[...]).astype(BF)


def finish_nodes(pre, nodes, w_out_ref, gain):
    projected = dot(silu(pre).astype(BF), w_out_ref[...])
    return (nodes.astype(F32) + layer_norm(projected) * gain).astype(BF)


def node_kernel(
    node_ref, sum_ref, w_in_ref, w_out_ref, gain_ref, edge_rows, _, out_ref, first_ref, pre_ref,
    new_ref, sem,
):
    copy = put_rows(edge_rows, new_ref, HALF, sem)
    nodes = node_ref[...]
    pre = dot(nodes, w_in_ref[:D])
    pre_ref[...] = pre[:TAIL]
    first_ref[...] = sum_ref[:TAIL]
    pre = pre + dot(sum_ref[...].astype(BF), w_in_ref[D:])
    out_ref[...] = finish_nodes(pre, nodes, w_out_ref, gain_ref[...])
    copy.wait()


def tail_kernel(
    node_ref, sum_ref, pre_ref, parts_ref, w_in_ref, w_out_ref, gain_ref, edge_rows, _, out_ref,
    new_ref, rows_ref, sems,
):
    edge_copy = put_rows(edge_rows, new_ref, 0, sems.at[0])
    parts = parts_ref[...].astype(F32).reshape(-1, COARSE_ROWS, D)
    total = sum_ref[...]
    total = jnp.concatenate(
        [total[:COARSE_ROWS] + jnp.sum(parts, axis=0), total[COARSE_ROWS:]], axis=0
    )
    pre = pre_ref[...] + dot(total.astype(BF), w_in_ref[D:])
    rows_ref[...] = finish_nodes(pre, node_ref[:TAIL], w_out_ref, gain_ref[...])
    put_rows(rows_ref, out_ref, 0, sems.at[1]).wait()
    edge_copy.wait()


def shape(rows, dtype=BF):
    return jax.ShapeDtypeStruct((rows, D), dtype)


VMEM_SPEC = pl.BlockSpec(memory_space=pltpu.VMEM)
ANY_SPEC = pl.BlockSpec(memory_space=pl.ANY)
HBM_SPEC = pl.BlockSpec(memory_space=pltpu.HBM)


def call(
    kernel, outs, flops, *args, name, scratch=(), out_any=(), in_any=(), aliases=None, spec=ANY_SPEC
):
    return pl.pallas_call(
        kernel,
        out_shape=outs,
        in_specs=[spec if at in in_any else VMEM_SPEC for at in range(len(args))],
        out_specs=tuple(
            ANY_SPEC if at in out_any else VMEM_SPEC for at in range(len(outs))
        ),
        scratch_shapes=scratch,
        input_output_aliases=aliases or {},
        compiler_params=pltpu.CompilerParams(vmem_limit_bytes=VMEM_LIMIT),
        cost_estimate=pl.CostEstimate(flops=flops, bytes_accessed=4 << 20, transcendentals=0),
        name=name,
    )(*args)


def patch_pairs(move):
    pairs = []
    for x in range(SIDE):
        for y in range(SIDE):
            for core in range(CORES):
                to_x, to_y, to_core = move(x, y, core)
                pairs.append(
                    ((x * SIDE + y) * CORES + core, (to_x * SIDE + to_y) * CORES + to_core)
                )
    return pairs


def crossed(k, turn):
    return patch_pairs(lambda x, y, c: (x ^ k, y, c) if c == turn else (x, y ^ k, c))


SWAP_CORE = patch_pairs(lambda x, y, c: (x, y, c ^ 1))


def along_z(move):
    pairs = []
    for group in range(GROUPS):
        pair, member = move(group >> 1, group & 1)
        target = ((pair % (GROUPS // 2)) << 1 | member) * PATCHES
        pairs += [(group * PATCHES + i, target + (i ^ 1)) for i in range(PATCHES)]
    return pairs


Z_PAIR = along_z(lambda pair, member: (pair, member ^ 1))
Z_FAR = along_z(lambda pair, member: (pair + 2, member ^ 1))
Z_MID = along_z(lambda pair, member: (pair - 1 + 2 * member, member))
Z_NEAR = along_z(lambda pair, member: (pair - 1 + 2 * member, member ^ 1))
OUTER = [(i, (i + 1 if i & 1 else i - 1) % PATCHES) for i in range(PATCHES)]
tie = lambda *arrays: lax.optimization_barrier(arrays)


def shards(
    node_lat, fine_edge_lat, fine_send, fine_recv, border_rows, coarse_edge_lat, coarse_send,
    coarse_recv, w_edge_in, w_edge_out, edge_gain, w_node_in, w_node_out, node_gain,
):
    edge_gain = edge_gain[None, :]
    node_gain = node_gain[None, :]
    grid = lambda ids: ids.reshape(-1, 128)
    swap = lambda rows, pairs: lax.ppermute(rows, "patch", pairs)
    join = lambda *rows: jnp.concatenate(rows, axis=0)

    in_hbm = lambda *arrays: [pltpu.with_memory_space_constraint(a, pltpu.HBM) for a in arrays]
    like = lambda *arrays: [jax.ShapeDtypeStruct(a.shape, a.dtype) for a in arrays]

    own = node_lat[:COARSE_ROWS]
    own, *loads = tie(own, border_rows, node_lat, w_edge_in)
    loads[0] = grid(loads[0])
    pair = lax.ppermute(own, ("group", "patch"), Z_PAIR)
    inner, outer, nodes, w_in = call(
        pick_kernel, [shape(BORDER), shape(BORDER), *like(*loads[1:])], 2 * 256 * 512 * 512,
        *in_hbm(*loads), name="pick",
        scratch=[pltpu.VMEM((2, BORDER), jnp.int32), pltpu.SemaphoreType.DMA((3,))],
        in_any=range(3), spec=HBM_SPEC,
    )
    pair, inner, outer, nodes, w_in = tie(pair, inner, outer, nodes, w_in)
    near = join(own, pair)
    near, inner, outer, nodes = tie(near, inner, outer, nodes)
    others = [lax.ppermute(near, ("group", "patch"), to) for to in (Z_NEAR, Z_MID, Z_FAR)]
    inner, outer = swap(inner, SWAP_CORE), swap(outer, OUTER)
    (table,) = call(
        project_kernel, (shape(2 * NODES),), 4 * 512 * 512 * 512, nodes, w_in, name="project"
    )
    *others, table = tie(*others, table)
    block = join(near, others[0], others[1], others[2])

    block, table = tie(block, table)
    others = [swap(block, crossed(k, 0)) for k in (1, 3, 2)]
    fine_args = (
        fine_edge_lat, grid(fine_send), grid(fine_recv), table, inner, outer, w_in, w_edge_out, edge_gain
    )
    rows, fine_sum, halo = call(
        functools.partial(fine_kernel, 0), (shape(HALF), shape(NODES, F32), shape(2 * BORDER)),
        2 << 30, *fine_args, name="fine_first",
    )
    *others, fine_sum = tie(*others, fine_sum)
    block = join(block, others[0], others[1], others[2])

    block, fine_sum = tie(block, fine_sum)
    others = [swap(block, crossed(k, 1)) for k in (1, 3, 2)]
    other_block = swap(block, SWAP_CORE)
    rows, fine_sum, fine_new = call(
        functools.partial(fine_kernel, HALF), (shape(HALF), shape(NODES, F32), shape(EDGES)),
        2 << 30, *fine_args, halo, fine_sum, rows, name="fine_second",
        scratch=[pltpu.SemaphoreType.DMA], out_any=(2,),
    )
    node_rows, first_sum, first_pre, fine_new = call(
        node_kernel, (shape(NODES), shape(TAIL, F32), shape(TAIL, F32), shape(EDGES)), 768 << 20,
        nodes, fine_sum, w_node_in, w_node_out, node_gain, rows, fine_new, name="node",
        scratch=[pltpu.SemaphoreType.DMA], out_any=(3,), in_any=(6,), aliases={6: 3},
    )
    other_block, first_sum = tie(other_block, first_sum)
    ids = jax.ShapeDtypeStruct((EDGES // 128, 128), jnp.int32)
    send_place, recv_place, send_part, recv_part, pre = call(
        early_kernel, (ids, ids, shape(EDGES), shape(EDGES), shape(EDGES, F32)), 2 << 30,
        coarse_edge_lat, grid(coarse_send), grid(coarse_recv), block, other_block, w_in,
        name="early", scratch=[pltpu.VMEM((2 * EARLY, D), BF)],
    )
    *others, pre = tie(*others, pre)
    part = join(others[0], others[1], others[2])
    other_part = swap(part, SWAP_CORE)
    send_part, recv_part, node_new = call(
        gather_kernel, (shape(EDGES), shape(EDGES), shape(NODES)), 2 << 30, send_place,
        recv_place, send_part, recv_part, part, node_rows, name="gather",
        scratch=[pltpu.SemaphoreType.DMA], out_any=(2,),
    )
    coarse_rows, sums = call(
        coarse_kernel, (shape(EDGES), shape(PATCHES * COARSE_ROWS)), 4 << 30, coarse_edge_lat,
        pre, send_place, recv_place, grid(coarse_recv), other_part, send_part, recv_part, w_in,
        w_edge_out, edge_gain, name="coarse",
        scratch=[pltpu.VMEM((EDGES // 128, 128), jnp.int32)],
    )

    parts = lax.all_to_all(sums.reshape(PATCHES, COARSE_ROWS, D), "patch", 0, 0)
    node_new, coarse_new = call(
        tail_kernel, (shape(NODES), shape(EDGES)), 24 << 20, nodes, first_sum, first_pre,
        parts.reshape(-1, D), w_node_in, w_node_out, node_gain, coarse_rows, node_new,
        name="tail", scratch=[pltpu.VMEM((TAIL, D), BF), pltpu.SemaphoreType.DMA((2,))],
        out_any=(0, 1), in_any=(8,), aliases={8: 0},
    )
    return (node_new, fine_new, coarse_new)


def solution(mesh):
    in_specs = (
        P(("group", "patch"), None), P(("group", "patch"), None), P(("group", "patch")),
        P(("group", "patch")), P(("group", "patch")), P("patch", None), P("patch"), P("patch"),
        P(), P(), P(), P(), P(), P(),
    )
    out_specs = (P(("group", "patch"), None), P(("group", "patch"), None), P("patch", None))
    return jax.shard_map(shards, mesh=mesh, in_specs=in_specs, out_specs=out_specs, check_vma=False)
```

```python
import functools

import jax
import jax.numpy as jnp
from jax import lax
from jax.experimental import pallas as pl
from jax.experimental.pallas import tpu as pltpu
from jax.sharding import PartitionSpec as P

D = 512
GROUPS = 8
SIDE = 4
CORES = 2
PATCHES = SIDE * SIDE * CORES
BORDER = 128
COARSE_ROWS = 8
EDGES = 1024
HALF = 512
EARLY = 256
NODES = 512
TAIL = 16
EPS = 1e-05
BF = jnp.bfloat16
F32 = jnp.float32
VMEM_LIMIT = 10 * 1024 * 1024


def dot(a, b):
    return jnp.dot(a, b, preferred_element_type=F32)


def silu(values):
    half = 0.5 * values
    return half * jnp.tanh(half) + half


def layer_norm(values):
    average = jnp.mean(values, axis=-1, keepdims=True)
    centred = values - average
    variance = jnp.mean(centred * centred, axis=-1, keepdims=True)
    return centred * lax.rsqrt(variance + EPS)


def column_of(ids_ref, first, rows):
    tiles = []
    for at in range(first // 128, (first + rows) // 128):
        row = jnp.broadcast_to(ids_ref[at : at + 1, :], (128, 128))
        tiles.append(row.T)
    return jnp.concatenate(tiles, axis=0).astype(jnp.int16)


def one_hot(column, width, offset=0):
    lanes = lax.broadcasted_iota(jnp.int16, column.shape, 1)
    one, zero = jnp.ones(column.shape, BF), jnp.zeros(column.shape, BF)
    return jnp.concatenate(
        [
            jnp.where(column == lanes + jnp.int16(offset + 128 * at), one, zero)
            for at in range(width // 128)
        ],
        axis=1,
    )


def one_hot_rows(ids_ref, first, count, height):
    rows = lax.broadcasted_iota(jnp.int16, (height, 128), 0)
    one, zero = jnp.ones((height, 128), BF), jnp.zeros((height, 128), BF)
    parts = []
    for at in range(first // 128, (first + count) // 128):
        ids = jnp.broadcast_to(ids_ref[at : at + 1, :], (height, 128)).astype(jnp.int16)
        parts.append(jnp.where(ids == rows, one, zero))
    return jnp.concatenate(parts, axis=1)


def put_rows(rows_ref, out_ref, first, sem):
    copy = pltpu.make_async_copy(rows_ref, out_ref.at[pl.ds(first, rows_ref.shape[0])], sem)
    copy.start()
    return copy


def finish_edges(pre, edges, w_out, gain):
    hidden = silu(pre).astype(BF)
    projected = dot(hidden, w_out)
    return (edges.astype(F32) + layer_norm(projected) * gain).astype(BF)


def pick_kernel(
    border_in, node_in, w_in, inner_ref, outer_ref, node_ref, w_in_ref, border_ref, sems
):
    copies = [
        pltpu.make_async_copy(source, target, sems.at[at])
        for at, (source, target) in enumerate(
            (
                (border_in, border_ref), (node_in, node_ref), (w_in, w_in_ref)
            )
        )
    ]
    for copy in copies:
        copy.start()
    copies[0].wait()
    hot = one_hot(column_of(border_ref, 0, 2 * BORDER), NODES)
    copies[1].wait()
    picked = dot(hot, node_ref[...]).astype(BF)
    lower, upper = picked[:BORDER], picked[BORDER:]
    on_first = lax.axis_index("patch") % CORES == 0
    inner_ref[...] = jnp.where(on_first, upper, lower)
    outer_ref[...] = jnp.where(on_first, lower, upper)
    for copy in copies[2:]:
        copy.wait()


def project_kernel(node_ref, w_ref, out_ref):
    nodes = node_ref[...]
    out_ref[:NODES] = dot(nodes, w_ref[2 * D :]).astype(BF)
    out_ref[NODES:] = dot(nodes, w_ref[D : 2 * D]).astype(BF)


def fine_kernel(
    first, edge_ref, send_ref, recv_ref, table_ref, inner_ref, outer_ref, w_in_ref, w_out_ref,
    gain_ref, *rest,
):
    if first:
        halo_in, before_ref, earlier_ref, rows_ref, sum_ref, new_ref, sem = rest
        copy = put_rows(earlier_ref, new_ref, 0, sem)
        halo = halo_in[...]
    else:
        rows_ref, sum_ref, halo_out = rest
        halo_out[:BORDER] = dot(inner_ref[...], w_in_ref[D : 2 * D]).astype(BF)
        halo_out[BORDER:] = dot(outer_ref[...], w_in_ref[D : 2 * D]).astype(BF)
        halo = halo_out[...]
    edges = edge_ref[first : first + HALF]
    senders = send_ref[...]
    on_first = lax.axis_index("patch") % CORES == 0
    senders = jnp.where((senders >= NODES) & on_first, senders ^ BORDER, senders)
    recv_hot = one_hot(column_of(recv_ref, first, HALF), NODES)
    send_hot = one_hot(column_of(senders, first, HALF), NODES + 2 * BORDER)
    pre = dot(edges, w_in_ref[:D])
    pre = pre + dot(jnp.concatenate([recv_hot, send_hot[:, :NODES]], axis=1), table_ref[...])
    pre = pre + dot(send_hot[:, NODES:], halo)
    rows_ref[...] = finish_edges(pre, edges, w_out_ref[...], gain_ref[...])
    sums = dot(one_hot_rows(recv_ref, first, HALF, NODES), rows_ref[...])
    sum_ref[...] = before_ref[...] + sums if first else sums
    if first:
        copy.wait()


def place_z(group, mine):
    away = ((group >> 1) - (mine >> 1)) * jnp.where(mine & 1 == 0, 1, -1) & 3
    high = away >> 1
    place = ((away ^ high) & 1) << 2 | high << 1 | ((group ^ mine) & 1 ^ high)
    return place, (place & 1) ^ jnp.where(place >= 2, 1, 0)


def place(ids):
    group, patch = lax.axis_index("group"), lax.axis_index("patch")
    my_core, my_y, my_x = patch & 1, patch >> 1 & 3, patch >> 3
    row, at = ids & 7, ids >> 3
    turn = lambda away: away ^ (away >> 1)
    core, y, x = at & 1, turn(at >> 1 & 3 ^ my_y), turn(at >> 3 & 3 ^ my_x)
    z, exchanged = place_z(at >> 5, group)
    half = core ^ my_core ^ exchanged
    x_first = half == my_core
    first, second = jnp.where(x_first, x, y), jnp.where(x_first, y, x)
    return half << 10 | second << 8 | first << 6 | z << 3 | row


def early_kernel(
    edge_ref, send_ref, recv_ref, mine_ref, theirs_ref, w_in_ref, send_place, recv_place,
    send_out, recv_out, pre_ref, table_ref,
):
    table_ref[:EARLY] = mine_ref[...]
    table_ref[EARLY:] = theirs_ref[...]
    pre_ref[...] = dot(edge_ref[...], w_in_ref[:D])
    for ids_ref, place_ref, out_ref in (
        (send_ref, send_place, send_out), (recv_ref, recv_place, recv_out)
    ):
        place_ref[...] = place(ids_ref[...])
        column = column_of(place_ref, 0, EDGES)
        hot = [one_hot(column, EARLY, first) for first in (0, SIDE * EARLY)]
        out_ref[...] = dot(jnp.concatenate(hot, axis=1), table_ref[...]).astype(BF)


def gather_kernel(
    send_ref, recv_ref, send_part, recv_part, table_ref, rows_ref, send_out, recv_out, new_ref, sem
):
    copy = put_rows(rows_ref, new_ref, 0, sem)
    for ids_ref, part_ref, out_ref in (
        (send_ref, send_part, send_out), (recv_ref, recv_part, recv_out)
    ):
        hot = one_hot(column_of(ids_ref, 0, EDGES), table_ref.shape[0], EARLY)
        out_ref[...] = (dot(hot, table_ref[...]) + part_ref[...].astype(F32)).astype(BF)
    copy.wait()


def coarse_kernel(
    edge_ref, pre_ref, send_ref, recv_ref, node_ref, table_ref, send_part, recv_part, w_in_ref,
    w_out_ref, gain_ref, rows_ref, sum_ref, slot_ref,
):
    joined = []
    for ids_ref, part_ref in ((send_ref, send_part), (recv_ref, recv_part)):
        hot = one_hot(column_of(ids_ref, 0, EDGES), table_ref.shape[0], (SIDE + 1) * EARLY)
        joined.append((dot(hot, table_ref[...]) + part_ref[...].astype(F32)).astype(BF))
    pre = pre_ref[...] + dot(jnp.concatenate(joined, axis=1), w_in_ref[D:])
    rows_ref[...] = finish_edges(pre, edge_ref[...], w_out_ref[...], gain_ref[...])
    nodes = node_ref[...]
    slot_ref[...] = jnp.where(nodes >> 8 == lax.axis_index("group"), nodes & 255, -1)
    hot = one_hot_rows(slot_ref, 0, EDGES, sum_ref.shape[0])
    sum_ref[...] = dot(hot, rows_ref[...]).astype(BF)


def finish_nodes(pre, nodes, w_out_ref, gain):
    projected = dot(silu(pre).astype(BF), w_out_ref[...])
    return (nodes.astype(F32) + layer_norm(projected) * gain).astype(BF)


def node_kernel(
    node_ref, sum_ref, w_in_ref, w_out_ref, gain_ref, edge_rows, coarse_ref, send_ref, recv_ref,
    mine_ref, theirs_ref, w_edge_ref, _, out_ref, first_ref, pre_ref, send_place, recv_place,
    send_out, recv_out, edge_pre_ref, new_ref, table_ref, sem,
):
    copy = put_rows(edge_rows, new_ref, HALF, sem)
    nodes = node_ref[...]
    pre = dot(nodes, w_in_ref[:D])
    pre_ref[...] = pre[:TAIL]
    first_ref[...] = sum_ref[:TAIL]
    pre = pre + dot(sum_ref[...].astype(BF), w_in_ref[D:])
    early_kernel(
        coarse_ref, send_ref, recv_ref, mine_ref, theirs_ref, w_edge_ref, send_place, recv_place,
        send_out, recv_out, edge_pre_ref, table_ref,
    )
    out_ref[...] = finish_nodes(pre, nodes, w_out_ref, gain_ref[...])
    copy.wait()


def tail_kernel(
    node_ref, sum_ref, pre_ref, parts_ref, w_in_ref, w_out_ref, gain_ref, edge_rows, _, out_ref,
    new_ref, rows_ref, sems,
):
    edge_copy = put_rows(edge_rows, new_ref, 0, sems.at[0])
    parts = parts_ref[...].astype(F32).reshape(-1, COARSE_ROWS, D)
    total = sum_ref[...]
    total = jnp.concatenate(
        [total[:COARSE_ROWS] + jnp.sum(parts, axis=0), total[COARSE_ROWS:]], axis=0
    )
    pre = pre_ref[...] + dot(total.astype(BF), w_in_ref[D:])
    rows_ref[...] = finish_nodes(pre, node_ref[:TAIL], w_out_ref, gain_ref[...])
    put_rows(rows_ref, out_ref, 0, sems.at[1]).wait()
    edge_copy.wait()


def shape(rows, dtype=BF):
    return jax.ShapeDtypeStruct((rows, D), dtype)


VMEM_SPEC = pl.BlockSpec(memory_space=pltpu.VMEM)
ANY_SPEC = pl.BlockSpec(memory_space=pl.ANY)
HBM_SPEC = pl.BlockSpec(memory_space=pltpu.HBM)


def call(
    kernel, outs, flops, *args, name, scratch=(), out_any=(), in_any=(), aliases=None, spec=ANY_SPEC
):
    return pl.pallas_call(
        kernel,
        out_shape=outs,
        in_specs=[spec if at in in_any else VMEM_SPEC for at in range(len(args))],
        out_specs=tuple(
            ANY_SPEC if at in out_any else VMEM_SPEC for at in range(len(outs))
        ),
        scratch_shapes=scratch,
        input_output_aliases=aliases or {},
        compiler_params=pltpu.CompilerParams(vmem_limit_bytes=VMEM_LIMIT),
        cost_estimate=pl.CostEstimate(flops=flops, bytes_accessed=4 << 20, transcendentals=0),
        name=name,
    )(*args)


def patch_pairs(move):
    pairs = []
    for x in range(SIDE):
        for y in range(SIDE):
            for core in range(CORES):
                to_x, to_y, to_core = move(x, y, core)
                pairs.append(
                    ((x * SIDE + y) * CORES + core, (to_x * SIDE + to_y) * CORES + to_core)
                )
    return pairs


def crossed(k, turn):
    return patch_pairs(lambda x, y, c: (x ^ k, y, c) if c == turn else (x, y ^ k, c))


SWAP_CORE = patch_pairs(lambda x, y, c: (x, y, c ^ 1))


def along_z(move):
    pairs = []
    for group in range(GROUPS):
        pair, member = move(group >> 1, group & 1)
        target = ((pair % (GROUPS // 2)) << 1 | member) * PATCHES
        pairs += [(group * PATCHES + i, target + (i ^ 1)) for i in range(PATCHES)]
    return pairs


Z_PAIR = along_z(lambda pair, member: (pair, member ^ 1))
Z_FAR = along_z(lambda pair, member: (pair + 2, member ^ 1))
Z_MID = along_z(lambda pair, member: (pair - 1 + 2 * member, member))
Z_NEAR = along_z(lambda pair, member: (pair - 1 + 2 * member, member ^ 1))
OUTER = [(i, (i + 1 if i & 1 else i - 1) % PATCHES) for i in range(PATCHES)]
tie = lambda *arrays: lax.optimization_barrier(arrays)


def shards(
    node_lat, fine_edge_lat, fine_send, fine_recv, border_rows, coarse_edge_lat, coarse_send,
    coarse_recv, w_edge_in, w_edge_out, edge_gain, w_node_in, w_node_out, node_gain,
):
    edge_gain = edge_gain[None, :]
    node_gain = node_gain[None, :]
    grid = lambda ids: ids.reshape(-1, 128)
    swap = lambda rows, pairs: lax.ppermute(rows, "patch", pairs)
    join = lambda *rows: jnp.concatenate(rows, axis=0)

    in_hbm = lambda *arrays: [pltpu.with_memory_space_constraint(a, pltpu.HBM) for a in arrays]
    like = lambda *arrays: [jax.ShapeDtypeStruct(a.shape, a.dtype) for a in arrays]

    own = node_lat[:COARSE_ROWS]
    own, *loads = tie(own, border_rows, node_lat, w_edge_in)
    loads[0] = grid(loads[0])
    pair = lax.ppermute(own, ("group", "patch"), Z_PAIR)
    inner, outer, nodes, w_in = call(
        pick_kernel, [shape(BORDER), shape(BORDER), *like(*loads[1:])], 2 * 256 * 512 * 512,
        *in_hbm(*loads), name="pick",
        scratch=[pltpu.VMEM((2, BORDER), jnp.int32), pltpu.SemaphoreType.DMA((3,))],
        in_any=range(3), spec=HBM_SPEC,
    )
    pair, inner, outer, nodes, w_in = tie(pair, inner, outer, nodes, w_in)
    near = join(own, pair)
    near, inner, outer, nodes = tie(near, inner, outer, nodes)
    others = [lax.ppermute(near, ("group", "patch"), to) for to in (Z_FAR, Z_MID, Z_NEAR)]
    inner, outer = swap(inner, SWAP_CORE), swap(outer, OUTER)
    (table,) = call(
        project_kernel, (shape(2 * NODES),), 4 * 512 * 512 * 512, nodes, w_in, name="project"
    )
    *others, table = tie(*others, table)
    block = join(near, *others[::-1])

    block, table = tie(block, table)
    others = [swap(block, crossed(k, 0)) for k in (2, 3, 1)]
    fine_args = (
        fine_edge_lat, grid(fine_send), grid(fine_recv), table, inner, outer, w_in, w_edge_out, edge_gain
    )
    rows, fine_sum, halo = call(
        functools.partial(fine_kernel, 0), (shape(HALF), shape(NODES, F32), shape(2 * BORDER)),
        2 << 30, *fine_args, name="fine_first",
    )
    *others, fine_sum = tie(*others, fine_sum)
    block = join(block, *others[::-1])

    block, fine_sum = tie(block, fine_sum)
    others = [swap(block, crossed(k, 1)) for k in (2, 3, 1)]
    other_block = swap(block, SWAP_CORE)
    rows, fine_sum, fine_new = call(
        functools.partial(fine_kernel, HALF), (shape(HALF), shape(NODES, F32), shape(EDGES)),
        2 << 30, *fine_args, halo, fine_sum, rows, name="fine_second",
        scratch=[pltpu.SemaphoreType.DMA], out_any=(2,),
    )
    ids = jax.ShapeDtypeStruct((EDGES // 128, 128), jnp.int32)
    (
        node_rows, first_sum, first_pre, send_place, recv_place, send_part, recv_part, pre,
        fine_new,
    ) = call(
        node_kernel,
        (
            shape(NODES), shape(TAIL, F32), shape(TAIL, F32), ids, ids, shape(EDGES),
            shape(EDGES), shape(EDGES, F32), shape(EDGES),
        ),
        3 << 30, nodes, fine_sum, w_node_in, w_node_out, node_gain, rows, coarse_edge_lat,
        grid(coarse_send), grid(coarse_recv), block, other_block, w_in, fine_new, name="node",
        scratch=[pltpu.VMEM((2 * EARLY, D), BF), pltpu.SemaphoreType.DMA], out_any=(8,),
        in_any=(12,), aliases={12: 8},
    )
    *others, pre = tie(*others, pre)
    part = join(*others[::-1])
    other_part = swap(part, SWAP_CORE)
    send_part, recv_part, node_new = call(
        gather_kernel, (shape(EDGES), shape(EDGES), shape(NODES)), 2 << 30, send_place,
        recv_place, send_part, recv_part, part, node_rows, name="gather",
        scratch=[pltpu.SemaphoreType.DMA], out_any=(2,),
    )
    coarse_rows, sums = call(
        coarse_kernel, (shape(EDGES), shape(PATCHES * COARSE_ROWS)), 4 << 30, coarse_edge_lat,
        pre, send_place, recv_place, grid(coarse_recv), other_part, send_part, recv_part, w_in,
        w_edge_out, edge_gain, name="coarse",
        scratch=[pltpu.VMEM((EDGES // 128, 128), jnp.int32)],
    )

    parts = lax.all_to_all(sums.reshape(PATCHES, COARSE_ROWS, D), "patch", 0, 0)
    node_new, coarse_new = call(
        tail_kernel, (shape(NODES), shape(EDGES)), 24 << 20, nodes, first_sum, first_pre,
        parts.reshape(-1, D), w_node_in, w_node_out, node_gain, coarse_rows, node_new,
        name="tail", scratch=[pltpu.VMEM((TAIL, D), BF), pltpu.SemaphoreType.DMA((2,))],
        out_any=(0, 1), in_any=(8,), aliases={8: 0},
    )
    return (node_new, fine_new, coarse_new)


def solution(mesh):
    in_specs = (
        P(("group", "patch"), None), P(("group", "patch"), None), P(("group", "patch")),
        P(("group", "patch")), P(("group", "patch")), P("patch", None), P("patch"), P("patch"),
        P(), P(), P(), P(), P(), P(),
    )
    out_specs = (P(("group", "patch"), None), P(("group", "patch"), None), P("patch", None))
    return jax.shard_map(shards, mesh=mesh, in_specs=in_specs, out_specs=out_specs, check_vma=False)
```

```python
import functools

import jax
import jax.numpy as jnp
from jax import lax
from jax.experimental import pallas as pl
from jax.experimental.pallas import tpu as pltpu
from jax.sharding import PartitionSpec as P

D = 512
GROUPS = 8
SIDE = 4
CORES = 2
PATCHES = SIDE * SIDE * CORES
BORDER = 128
COARSE_ROWS = 8
EDGES = 1024
HALF = 512
EARLY = 256
NODES = 512
TAIL = 16
EPS = 1e-05
BF = jnp.bfloat16
F32 = jnp.float32
VMEM_LIMIT = 10 * 1024 * 1024


def dot(a, b):
    return jnp.dot(a, b, preferred_element_type=F32)


def silu(values):
    half = 0.5 * values
    return half * jnp.tanh(half) + half


def layer_norm(values):
    average = jnp.mean(values, axis=-1, keepdims=True)
    centred = values - average
    variance = jnp.mean(centred * centred, axis=-1, keepdims=True)
    return centred * lax.rsqrt(variance + EPS)


def column_of(ids_ref, first, rows):
    tiles = []
    for at in range(first // 128, (first + rows) // 128):
        row = jnp.broadcast_to(ids_ref[at : at + 1, :], (128, 128))
        tiles.append(row.T)
    return jnp.concatenate(tiles, axis=0).astype(jnp.int16)


def one_hot(column, width, offset=0):
    lanes = lax.broadcasted_iota(jnp.int16, column.shape, 1)
    one, zero = jnp.ones(column.shape, BF), jnp.zeros(column.shape, BF)
    return jnp.concatenate(
        [
            jnp.where(column == lanes + jnp.int16(offset + 128 * at), one, zero)
            for at in range(width // 128)
        ],
        axis=1,
    )


def one_hot_rows(ids_ref, first, count, height):
    rows = lax.broadcasted_iota(jnp.int16, (height, 128), 0)
    one, zero = jnp.ones((height, 128), BF), jnp.zeros((height, 128), BF)
    parts = []
    for at in range(first // 128, (first + count) // 128):
        ids = jnp.broadcast_to(ids_ref[at : at + 1, :], (height, 128)).astype(jnp.int16)
        parts.append(jnp.where(ids == rows, one, zero))
    return jnp.concatenate(parts, axis=1)


def put_rows(rows_ref, out_ref, first, sem):
    copy = pltpu.make_async_copy(rows_ref, out_ref.at[pl.ds(first, rows_ref.shape[0])], sem)
    copy.start()
    return copy


def finish_edges(pre, edges, w_out, gain):
    hidden = silu(pre).astype(BF)
    projected = dot(hidden, w_out)
    return (edges.astype(F32) + layer_norm(projected) * gain).astype(BF)


def pick_kernel(
    border_in, node_in, w_in, inner_ref, outer_ref, node_ref, w_in_ref, border_ref, sems
):
    copies = [
        pltpu.make_async_copy(source, target, sems.at[at])
        for at, (source, target) in enumerate(
            (
                (border_in, border_ref), (node_in, node_ref), (w_in, w_in_ref)
            )
        )
    ]
    for copy in copies:
        copy.start()
    copies[0].wait()
    hot = one_hot(column_of(border_ref, 0, 2 * BORDER), NODES)
    copies[1].wait()
    picked = dot(hot, node_ref[...]).astype(BF)
    lower, upper = picked[:BORDER], picked[BORDER:]
    on_first = lax.axis_index("patch") % CORES == 0
    inner_ref[...] = jnp.where(on_first, upper, lower)
    outer_ref[...] = jnp.where(on_first, lower, upper)
    for copy in copies[2:]:
        copy.wait()


def project_kernel(node_ref, w_ref, edge_ref, out_ref, edge_pre_ref):
    edge_pre_ref[...] = dot(edge_ref[...], w_ref[:D])
    nodes = node_ref[...]
    out_ref[:NODES] = dot(nodes, w_ref[2 * D :]).astype(BF)
    out_ref[NODES:] = dot(nodes, w_ref[D : 2 * D]).astype(BF)


def fine_kernel(
    first, edge_ref, send_ref, recv_ref, table_ref, inner_ref, outer_ref, w_in_ref, w_out_ref,
    gain_ref, *rest,
):
    if first:
        halo_in, before_ref, earlier_ref, rows_ref, sum_ref, new_ref, sem = rest
        copy = put_rows(earlier_ref, new_ref, 0, sem)
        halo = halo_in[...]
    else:
        rows_ref, sum_ref, halo_out = rest
        halo_out[:BORDER] = dot(inner_ref[...], w_in_ref[D : 2 * D]).astype(BF)
        halo_out[BORDER:] = dot(outer_ref[...], w_in_ref[D : 2 * D]).astype(BF)
        halo = halo_out[...]
    edges = edge_ref[first : first + HALF]
    senders = send_ref[...]
    on_first = lax.axis_index("patch") % CORES == 0
    senders = jnp.where((senders >= NODES) & on_first, senders ^ BORDER, senders)
    recv_hot = one_hot(column_of(recv_ref, first, HALF), NODES)
    send_hot = one_hot(column_of(senders, first, HALF), NODES + 2 * BORDER)
    pre = dot(edges, w_in_ref[:D])
    pre = pre + dot(jnp.concatenate([recv_hot, send_hot[:, :NODES]], axis=1), table_ref[...])
    pre = pre + dot(send_hot[:, NODES:], halo)
    rows_ref[...] = finish_edges(pre, edges, w_out_ref[...], gain_ref[...])
    sums = dot(one_hot_rows(recv_ref, first, HALF, NODES), rows_ref[...])
    sum_ref[...] = before_ref[...] + sums if first else sums
    if first:
        copy.wait()


def place_z(group, mine):
    away = ((group >> 1) - (mine >> 1)) * jnp.where(mine & 1 == 0, 1, -1) & 3
    high = away >> 1
    place = ((away ^ high) & 1) << 2 | high << 1 | ((group ^ mine) & 1 ^ high)
    return place, (place & 1) ^ jnp.where(place >= 2, 1, 0)


def place(ids):
    group, patch = lax.axis_index("group"), lax.axis_index("patch")
    my_core, my_y, my_x = patch & 1, patch >> 1 & 3, patch >> 3
    row, at = ids & 7, ids >> 3
    turn = lambda away: away ^ (away >> 1)
    core, y, x = at & 1, turn(at >> 1 & 3 ^ my_y), turn(at >> 3 & 3 ^ my_x)
    z, exchanged = place_z(at >> 5, group)
    half = core ^ my_core ^ exchanged
    x_first = half == my_core
    first, second = jnp.where(x_first, x, y), jnp.where(x_first, y, x)
    return half << 10 | second << 8 | first << 6 | z << 3 | row


def early_kernel(
    send_ref, recv_ref, mine_ref, theirs_ref, send_place, recv_place, send_out, recv_out,
    table_ref,
):
    table_ref[:EARLY] = mine_ref[...]
    table_ref[EARLY:] = theirs_ref[...]
    for ids_ref, place_ref, out_ref in (
        (send_ref, send_place, send_out), (recv_ref, recv_place, recv_out)
    ):
        place_ref[...] = place(ids_ref[...])
        column = column_of(place_ref, 0, EDGES)
        hot = [one_hot(column, EARLY, first) for first in (0, SIDE * EARLY)]
        out_ref[...] = dot(jnp.concatenate(hot, axis=1), table_ref[...]).astype(BF)


def gather_kernel(
    send_ref, recv_ref, send_part, recv_part, table_ref, rows_ref, send_out, recv_out, new_ref, sem
):
    copy = put_rows(rows_ref, new_ref, 0, sem)
    for ids_ref, part_ref, out_ref in (
        (send_ref, send_part, send_out), (recv_ref, recv_part, recv_out)
    ):
        hot = one_hot(column_of(ids_ref, 0, EDGES), table_ref.shape[0], EARLY)
        out_ref[...] = (dot(hot, table_ref[...]) + part_ref[...].astype(F32)).astype(BF)
    copy.wait()


def coarse_kernel(
    edge_ref, pre_ref, send_ref, recv_ref, node_ref, table_ref, send_part, recv_part, w_in_ref,
    w_out_ref, gain_ref, rows_ref, sum_ref, slot_ref,
):
    joined = []
    for ids_ref, part_ref in ((send_ref, send_part), (recv_ref, recv_part)):
        hot = one_hot(column_of(ids_ref, 0, EDGES), table_ref.shape[0], (SIDE + 1) * EARLY)
        joined.append((dot(hot, table_ref[...]) + part_ref[...].astype(F32)).astype(BF))
    pre = pre_ref[...] + dot(jnp.concatenate(joined, axis=1), w_in_ref[D:])
    rows_ref[...] = finish_edges(pre, edge_ref[...], w_out_ref[...], gain_ref[...])
    nodes = node_ref[...]
    slot_ref[...] = jnp.where(nodes >> 8 == lax.axis_index("group"), nodes & 255, -1)
    hot = one_hot_rows(slot_ref, 0, EDGES, sum_ref.shape[0])
    sum_ref[...] = dot(hot, rows_ref[...]).astype(BF)


def finish_nodes(pre, nodes, w_out_ref, gain):
    projected = dot(silu(pre).astype(BF), w_out_ref[...])
    return (nodes.astype(F32) + layer_norm(projected) * gain).astype(BF)


def node_kernel(
    node_ref, sum_ref, w_in_ref, w_out_ref, gain_ref, edge_rows, _, out_ref, first_ref, pre_ref,
    new_ref, sem,
):
    copy = put_rows(edge_rows, new_ref, HALF, sem)
    nodes = node_ref[...]
    pre = dot(nodes, w_in_ref[:D])
    pre_ref[...] = pre[:TAIL]
    first_ref[...] = sum_ref[:TAIL]
    pre = pre + dot(sum_ref[...].astype(BF), w_in_ref[D:])
    out_ref[...] = finish_nodes(pre, nodes, w_out_ref, gain_ref[...])
    copy.wait()


def tail_kernel(
    node_ref, sum_ref, pre_ref, parts_ref, w_in_ref, w_out_ref, gain_ref, edge_rows, _, out_ref,
    new_ref, rows_ref, sems,
):
    edge_copy = put_rows(edge_rows, new_ref, 0, sems.at[0])
    parts = parts_ref[...].astype(F32).reshape(-1, COARSE_ROWS, D)
    total = sum_ref[...]
    total = jnp.concatenate(
        [total[:COARSE_ROWS] + jnp.sum(parts, axis=0), total[COARSE_ROWS:]], axis=0
    )
    pre = pre_ref[...] + dot(total.astype(BF), w_in_ref[D:])
    rows_ref[...] = finish_nodes(pre, node_ref[:TAIL], w_out_ref, gain_ref[...])
    put_rows(rows_ref, out_ref, 0, sems.at[1]).wait()
    edge_copy.wait()


def shape(rows, dtype=BF):
    return jax.ShapeDtypeStruct((rows, D), dtype)


VMEM_SPEC = pl.BlockSpec(memory_space=pltpu.VMEM)
ANY_SPEC = pl.BlockSpec(memory_space=pl.ANY)
HBM_SPEC = pl.BlockSpec(memory_space=pltpu.HBM)


def call(
    kernel, outs, flops, *args, name, scratch=(), out_any=(), in_any=(), aliases=None, spec=ANY_SPEC
):
    return pl.pallas_call(
        kernel,
        out_shape=outs,
        in_specs=[spec if at in in_any else VMEM_SPEC for at in range(len(args))],
        out_specs=tuple(
            ANY_SPEC if at in out_any else VMEM_SPEC for at in range(len(outs))
        ),
        scratch_shapes=scratch,
        input_output_aliases=aliases or {},
        compiler_params=pltpu.CompilerParams(vmem_limit_bytes=VMEM_LIMIT),
        cost_estimate=pl.CostEstimate(flops=flops, bytes_accessed=4 << 20, transcendentals=0),
        name=name,
    )(*args)


def patch_pairs(move):
    pairs = []
    for x in range(SIDE):
        for y in range(SIDE):
            for core in range(CORES):
                to_x, to_y, to_core = move(x, y, core)
                pairs.append(
                    ((x * SIDE + y) * CORES + core, (to_x * SIDE + to_y) * CORES + to_core)
                )
    return pairs


def crossed(k, turn):
    return patch_pairs(lambda x, y, c: (x ^ k, y, c) if c == turn else (x, y ^ k, c))


SWAP_CORE = patch_pairs(lambda x, y, c: (x, y, c ^ 1))


def along_z(move):
    pairs = []
    for group in range(GROUPS):
        pair, member = move(group >> 1, group & 1)
        target = ((pair % (GROUPS // 2)) << 1 | member) * PATCHES
        pairs += [(group * PATCHES + i, target + (i ^ 1)) for i in range(PATCHES)]
    return pairs


Z_PAIR = along_z(lambda pair, member: (pair, member ^ 1))
Z_FAR = along_z(lambda pair, member: (pair + 2, member ^ 1))
Z_MID = along_z(lambda pair, member: (pair - 1 + 2 * member, member))
Z_NEAR = along_z(lambda pair, member: (pair - 1 + 2 * member, member ^ 1))
OUTER = [(i, (i + 1 if i & 1 else i - 1) % PATCHES) for i in range(PATCHES)]
tie = lambda *arrays: lax.optimization_barrier(arrays)


def shards(
    node_lat, fine_edge_lat, fine_send, fine_recv, border_rows, coarse_edge_lat, coarse_send,
    coarse_recv, w_edge_in, w_edge_out, edge_gain, w_node_in, w_node_out, node_gain,
):
    edge_gain = edge_gain[None, :]
    node_gain = node_gain[None, :]
    grid = lambda ids: ids.reshape(-1, 128)
    swap = lambda rows, pairs: lax.ppermute(rows, "patch", pairs)
    join = lambda *rows: jnp.concatenate(rows, axis=0)

    in_hbm = lambda *arrays: [pltpu.with_memory_space_constraint(a, pltpu.HBM) for a in arrays]
    like = lambda *arrays: [jax.ShapeDtypeStruct(a.shape, a.dtype) for a in arrays]

    own = node_lat[:COARSE_ROWS]
    own, *loads = tie(own, border_rows, node_lat, w_edge_in)
    loads[0] = grid(loads[0])
    pair = lax.ppermute(own, ("group", "patch"), Z_PAIR)
    inner, outer, nodes, w_in = call(
        pick_kernel, [shape(BORDER), shape(BORDER), *like(*loads[1:])], 2 * 256 * 512 * 512,
        *in_hbm(*loads), name="pick",
        scratch=[pltpu.VMEM((2, BORDER), jnp.int32), pltpu.SemaphoreType.DMA((3,))],
        in_any=range(3), spec=HBM_SPEC,
    )
    pair, inner, outer, nodes, w_in = tie(pair, inner, outer, nodes, w_in)
    near = join(own, pair)
    near, inner, outer, nodes = tie(near, inner, outer, nodes)
    others = [lax.ppermute(near, ("group", "patch"), to) for to in (Z_NEAR, Z_MID, Z_FAR)]
    inner, outer = swap(inner, SWAP_CORE), swap(outer, OUTER)
    table, pre = call(
        project_kernel, (shape(2 * NODES), shape(EDGES, F32)), 1 << 30, nodes, w_in,
        coarse_edge_lat, name="project",
    )
    *others, table = tie(*others, table)
    block = join(near, others[0], others[1], others[2])

    block, table = tie(block, table)
    others = [swap(block, crossed(k, 0)) for k in (1, 3, 2)]
    fine_args = (
        fine_edge_lat, grid(fine_send), grid(fine_recv), table, inner, outer, w_in, w_edge_out, edge_gain
    )
    rows, fine_sum, halo = call(
        functools.partial(fine_kernel, 0), (shape(HALF), shape(NODES, F32), shape(2 * BORDER)),
        2 << 30, *fine_args, name="fine_first",
    )
    *others, fine_sum = tie(*others, fine_sum)
    block = join(block, others[0], others[1], others[2])

    block, fine_sum = tie(block, fine_sum)
    others = [swap(block, crossed(k, 1)) for k in (1, 3, 2)]
    other_block = swap(block, SWAP_CORE)
    rows, fine_sum, fine_new = call(
        functools.partial(fine_kernel, HALF), (shape(HALF), shape(NODES, F32), shape(EDGES)),
        2 << 30, *fine_args, halo, fine_sum, rows, name="fine_second",
        scratch=[pltpu.SemaphoreType.DMA], out_any=(2,),
    )
    node_rows, first_sum, first_pre, fine_new = call(
        node_kernel, (shape(NODES), shape(TAIL, F32), shape(TAIL, F32), shape(EDGES)), 768 << 20,
        nodes, fine_sum, w_node_in, w_node_out, node_gain, rows, fine_new, name="node",
        scratch=[pltpu.SemaphoreType.DMA], out_any=(3,), in_any=(6,), aliases={6: 3},
    )
    other_block, first_sum = tie(other_block, first_sum)
    ids = jax.ShapeDtypeStruct((EDGES // 128, 128), jnp.int32)
    send_place, recv_place, send_part, recv_part = call(
        early_kernel, (ids, ids, shape(EDGES), shape(EDGES)), 2 << 30, grid(coarse_send),
        grid(coarse_recv), block, other_block,
        name="early", scratch=[pltpu.VMEM((2 * EARLY, D), BF)],
    )
    *others, send_part = tie(*others, send_part)
    part = join(others[0], others[1], others[2])
    other_part = swap(part, SWAP_CORE)
    send_part, recv_part, node_new = call(
        gather_kernel, (shape(EDGES), shape(EDGES), shape(NODES)), 2 << 30, send_place,
        recv_place, send_part, recv_part, part, node_rows, name="gather",
        scratch=[pltpu.SemaphoreType.DMA], out_any=(2,),
    )
    coarse_rows, sums = call(
        coarse_kernel, (shape(EDGES), shape(PATCHES * COARSE_ROWS)), 4 << 30, coarse_edge_lat,
        pre, send_place, recv_place, grid(coarse_recv), other_part, send_part, recv_part, w_in,
        w_edge_out, edge_gain, name="coarse",
        scratch=[pltpu.VMEM((EDGES // 128, 128), jnp.int32)],
    )

    parts = lax.all_to_all(sums.reshape(PATCHES, COARSE_ROWS, D), "patch", 0, 0)
    node_new, coarse_new = call(
        tail_kernel, (shape(NODES), shape(EDGES)), 24 << 20, nodes, first_sum, first_pre,
        parts.reshape(-1, D), w_node_in, w_node_out, node_gain, coarse_rows, node_new,
        name="tail", scratch=[pltpu.VMEM((TAIL, D), BF), pltpu.SemaphoreType.DMA((2,))],
        out_any=(0, 1), in_any=(8,), aliases={8: 0},
    )
    return (node_new, fine_new, coarse_new)


def solution(mesh):
    in_specs = (
        P(("group", "patch"), None), P(("group", "patch"), None), P(("group", "patch")),
        P(("group", "patch")), P(("group", "patch")), P("patch", None), P("patch"), P("patch"),
        P(), P(), P(), P(), P(), P(),
    )
    out_specs = (P(("group", "patch"), None), P(("group", "patch"), None), P("patch", None))
    return jax.shard_map(shards, mesh=mesh, in_specs=in_specs, out_specs=out_specs, check_vma=False)
```
